256 devices in a mesh: slide: 4 (over x_hi, core), seq: 64 (over z, x_lo, y).
Axes of the slice: x: 4 (x_hi: 2, x_lo: 2; x = x_hi * 2 + x_lo), y: 4, z: 8, core: 2. Of those that a mesh axis runs over, the one named last changes fastest.
Arguments:
- query_rows: bfloat16 [4, 16384, 768], P('slide', 'seq'), may hold values from -270 to 270
- key_rows: bfloat16 [4, 16384, 768], P('slide', 'seq'), may hold values from -6 to 6
- value_rows: bfloat16 [4, 16384, 768], P('slide', 'seq'), may hold values from -6 to 6
- grad_out: bfloat16 [4, 16384, 768], P('slide', 'seq'), may hold values from -6 to 6
- out_weight: bfloat16 [768, 768], replicated, may hold values from -0.21875 to 0.21875
- tile_counts: int32 [4], P('slide'), may hold values from 4096 to 16384, as said below
Outputs:
- layer_out: bfloat16 [4, 16384, 768], P('slide', 'seq')
- grad_query: bfloat16 [4, 16384, 768], P('slide', 'seq')
- grad_key: bfloat16 [4, 16384, 768], P('slide', 'seq')
- grad_value: bfloat16 [4, 16384, 768], P('slide', 'seq')
- grad_weight: float32 [768, 768], P('seq')
The draws below stay inside these ranges and needn't reach their ends.
Inputs may be any that keep to these rules, and one draw needn't show every extreme that they name: Positions 0 to tile_counts - 1 of a slide are valid; in every draw one slide has all 16384 positions valid.
All inputs are finite; a program needn't handle non-finite values.
Results may differ from the reference program's by a relative error of at most 0.0095.
Values may be sent and summed in bfloat16 or wider, within the bound.
No kernel may reach another device: no remote copies, remote signals or barrier semaphores. Data moves between devices by JAX's collectives and lax.ppermute only.
A program may use at most 128 MiB of HBM per device.

```python
import jax
import jax.numpy as jnp
from jax import lax

HEADS = 16
D = 768
TOK_DEV = 256
DILATION_FACTOR = 16
SEQ_LEN = 16384
SLIDES = 4
N_SEQ = 64


def shared_keys(key):
    return jnp.clip(jax.random.normal(key, (SLIDES, SEQ_LEN, D), jnp.float32), -6.0, 6.0)


def draw_key_rows(key, part):
    return shared_keys(key).astype(jnp.bfloat16)


def draw_query_rows(key, part):
    key = jax.random.fold_in(key, 7)
    fresh = jnp.clip(jax.random.normal(key, (SLIDES, SEQ_LEN, D), jnp.float32), -6.0, 6.0)
    return fresh.astype(jnp.bfloat16)


def draw_tile_counts(key, part):
    key = jax.random.fold_in(key, 5)
    counts = jax.random.randint(key, (SLIDES,), SEQ_LEN // 4, SEQ_LEN + 1, dtype=jnp.int32)
    chosen = jax.random.randint(jax.random.fold_in(key, 9), (), 0, SLIDES, dtype=jnp.int32)
    return jnp.where(jnp.arange(SLIDES, dtype=jnp.int32) == chosen, SEQ_LEN, counts).astype(jnp.int32)


def block_scale(own_key, shape, cuts, least, largest):
    def one(position, blocks):
        draws = jax.random.uniform(jax.random.fold_in(jax.random.fold_in(own_key, 6), position), (blocks,), jnp.float32, least / len(cuts), largest / len(cuts))
        return jnp.repeat(jnp.exp(draws), shape[position] // blocks).reshape((-1,) + (1,) * (len(shape) - position - 1))

    loudness = one(*cuts[0])
    for cut in cuts[1:]:
        loudness = loudness * one(*cut)
    return loudness


def centred(rng, shape, width, limit, split=(), kind=jnp.bfloat16):
    values = width * jax.random.normal(rng, shape, jnp.float32)
    if split:
        values = values * block_scale(rng, shape, split, -0.22, 0.18)
    return jnp.clip(values, -limit, limit).astype(kind)


def setup_inputs(seed: int = 0) -> dict:
    keys = jax.random.split(jax.random.key(seed), 7)
    return {
        "query_rows": draw_query_rows(jax.random.fold_in(keys[6], 71), 0),
        "key_rows": draw_key_rows(jax.random.fold_in(keys[6], 71), 0),
        "value_rows": centred(keys[2], (SLIDES, SEQ_LEN, D), 1.0, 6.0, ((0, 4), (1, 64))),
        "grad_out": centred(keys[3], (SLIDES, SEQ_LEN, D), 1.0, 6.0, ((0, 4), (1, 64))),
        "out_weight": centred(keys[4], (D, D), D ** -0.5, 0.21875),
        "tile_counts": draw_tile_counts(jax.random.fold_in(keys[6], 71), 0),
    }


masked_score = -1e30


def strided_flags(head_count):
    return jnp.arange(DILATION_FACTOR, dtype=jnp.int32)[None, :] == (jnp.arange(head_count, dtype=jnp.int32) % DILATION_FACTOR)[:, None]


def dilate(input_matrix, head_count):
    count_of_rows, feature_width = input_matrix.shape
    blocked_layout = input_matrix.reshape(count_of_rows // DILATION_FACTOR, DILATION_FACTOR, head_count, feature_width // head_count)
    chosen = strided_flags(head_count).T[None, :, :, None]
    return jnp.sum(jnp.where(chosen, blocked_layout, jnp.zeros((), input_matrix.dtype)), axis=1).astype(input_matrix.dtype)


def undilate(strided_tensor, head_count):
    chosen = strided_flags(head_count).T[None, :, :, None]
    spread_rows = jnp.where(chosen, strided_tensor[:, None, :, :], jnp.zeros((), strided_tensor.dtype))
    return spread_rows.reshape(strided_tensor.shape[0] * DILATION_FACTOR, strided_tensor.shape[1], strided_tensor.shape[2])


def select_strided(softmax_statistic, head_count):
    blocked_layout = softmax_statistic.reshape(softmax_statistic.shape[0], softmax_statistic.shape[1] // DILATION_FACTOR, DILATION_FACTOR)
    return jnp.sum(jnp.where(strided_flags(head_count)[:, None, :], blocked_layout, jnp.zeros((), softmax_statistic.dtype)), axis=-1)


def spread_stat(strided_tensor, full_tensor, head_count):
    blocked_layout = full_tensor.reshape(full_tensor.shape[0], full_tensor.shape[1] // DILATION_FACTOR, DILATION_FACTOR)
    return jnp.where(strided_flags(head_count)[:, None, :], strided_tensor[:, :, None], blocked_layout).reshape(full_tensor.shape)


def product(form, left, right):
    return jnp.einsum(form, left.astype(jnp.float32), right.astype(jnp.float32))


def segment(queries, keys_local, values_local, grad_rows, out_weight, k_global, v_global, row_start, tile_count):
    count_of_rows, feature_width = queries.shape
    head_count = HEADS
    head_width = feature_width // head_count
    score_scale = head_width ** -0.5
    slide_wide_rows = k_global.shape[0]
    valid_rows = (row_start + jnp.arange(count_of_rows, dtype=jnp.int32)) < tile_count
    q_heads = queries.reshape(count_of_rows, head_count, head_width)
    k_heads = keys_local.reshape(count_of_rows, head_count, head_width)
    v_heads = values_local.reshape(count_of_rows, head_count, head_width)
    q_strided = dilate(queries, head_count)
    global_position = jnp.arange(slide_wide_rows, dtype=jnp.int32)[None, :] * DILATION_FACTOR + (jnp.arange(head_count, dtype=jnp.int32) % DILATION_FACTOR)[:, None]
    scores_near = product('qhd,khd->hqk', q_heads, k_heads) * score_scale
    scores_near = jnp.where(valid_rows[None, None, :], scores_near, masked_score)
    scores_far = product('qhd,khd->hqk', q_strided, k_global) * score_scale
    scores_far = jnp.where((global_position < tile_count)[:, None, :], scores_far, masked_score)
    max_near = jnp.max(scores_near, axis=-1)
    max_far = jnp.max(scores_far, axis=-1)
    max_strided = jnp.maximum(max_far, select_strided(max_near, head_count))
    max_rows = spread_stat(max_strided, max_near, head_count)
    exp_near = jnp.exp(scores_near - max_rows[:, :, None])
    exp_far = jnp.exp(scores_far - max_strided[:, :, None])
    sum_near = jnp.sum(exp_near, axis=-1)
    sum_rows = sum_near + spread_stat(jnp.sum(exp_far, axis=-1), jnp.zeros_like(sum_near), head_count)
    sum_strided = select_strided(sum_rows, head_count)
    accum = product('hqk,khd->qhd', exp_near.astype(jnp.bfloat16), v_heads)
    accum = accum + undilate(product('hqk,khd->qhd', exp_far.astype(jnp.bfloat16), v_global), head_count)
    out_heads = (accum / sum_rows.T[:, :, None]).astype(jnp.bfloat16)
    attended = out_heads.reshape(count_of_rows, feature_width)
    layer_out = jnp.where(valid_rows[:, None], jnp.dot(attended, out_weight, preferred_element_type=jnp.float32), 0.0).astype(jnp.bfloat16)
    grad_masked = jnp.where(valid_rows[:, None], grad_rows, jnp.zeros((), grad_rows.dtype))
    d_attended = jnp.dot(grad_masked, out_weight.T, preferred_element_type=jnp.float32).astype(jnp.bfloat16)
    grad_heads = d_attended.reshape(count_of_rows, head_count, head_width)
    delta_rows = jnp.sum(grad_heads.astype(jnp.float32) * out_heads.astype(jnp.float32), axis=-1).T
    delta_strided = select_strided(delta_rows, head_count)
    grad_strided = dilate(d_attended, head_count)
    prob_near = exp_near / sum_rows[:, :, None]
    dprob_near = product('qhd,khd->hqk', grad_heads, v_heads)
    dscore_near = (prob_near * (dprob_near - delta_rows[:, :, None])).astype(jnp.bfloat16)
    grad_q = product('hqk,khd->qhd', dscore_near, k_heads) * score_scale
    grad_k = product('hqk,qhd->khd', dscore_near, q_heads) * score_scale
    grad_v = product('hqk,qhd->khd', prob_near.astype(jnp.bfloat16), grad_heads)
    prob_far = exp_far / sum_strided[:, :, None]
    dprob_far = product('qhd,khd->hqk', grad_strided, v_global)
    dscore_far = (prob_far * (dprob_far - delta_strided[:, :, None])).astype(jnp.bfloat16)
    grad_q = grad_q + undilate(product('hqk,khd->qhd', dscore_far, k_global) * score_scale, head_count)
    far_key = product('hqk,qhd->khd', dscore_far, q_strided) * score_scale
    far_value = product('hqk,qhd->khd', prob_far.astype(jnp.bfloat16), grad_strided)
    return layer_out, attended, grad_masked, grad_q, grad_k, grad_v, far_key, far_value


def reference(query_rows, key_rows, value_rows, grad_out, out_weight, tile_counts):
    head_count = HEADS
    feature_width = query_rows.shape[2]
    head_width = feature_width // head_count
    outs_layer, outs_query, outs_key, outs_value = [], [], [], []
    all_attended, all_grad = [], []
    for slide_index in range(SLIDES):
        queries = query_rows[slide_index]
        keys_all = key_rows[slide_index]
        values_all = value_rows[slide_index]
        grads_all = grad_out[slide_index]
        tile_count = tile_counts[slide_index]
        k_global = dilate(keys_all, head_count)
        v_global = dilate(values_all, head_count)

        def segment_step(totals, segment_index):
            row_start = (segment_index * TOK_DEV).astype(jnp.int32)
            pieces = [lax.dynamic_slice_in_dim(array, row_start, TOK_DEV, 0) for array in (queries, keys_all, values_all, grads_all)]
            result = segment(pieces[0], pieces[1], pieces[2], pieces[3], out_weight, k_global, v_global, row_start, tile_count)
            return (totals[0] + result[6], totals[1] + result[7]), result[:6]

        start_totals = (jnp.zeros(k_global.shape, jnp.float32), jnp.zeros(k_global.shape, jnp.float32))
        (far_key, far_value), stacked = lax.scan(segment_step, start_totals, jnp.arange(N_SEQ, dtype=jnp.int32))
        layer_out, attended, grad_masked, grad_q, grad_k, grad_v = stacked
        outs_layer.append(layer_out.reshape(SEQ_LEN, feature_width))
        all_attended.append(attended.reshape(SEQ_LEN, feature_width))
        all_grad.append(grad_masked.reshape(SEQ_LEN, feature_width))
        outs_query.append(grad_q.reshape(SEQ_LEN, feature_width).astype(jnp.bfloat16))
        full_key = grad_k.reshape(SEQ_LEN, head_count, head_width) + undilate(far_key, head_count)
        full_value = grad_v.reshape(SEQ_LEN, head_count, head_width) + undilate(far_value, head_count)
        outs_key.append(full_key.reshape(SEQ_LEN, feature_width).astype(jnp.bfloat16))
        outs_value.append(full_value.reshape(SEQ_LEN, feature_width).astype(jnp.bfloat16))
    attended_cat = jnp.concatenate(all_attended, axis=0)
    grad_cat = jnp.concatenate(all_grad, axis=0)
    grad_weight = jnp.dot(attended_cat.T, grad_cat, preferred_element_type=jnp.float32)
    return (jnp.stack(outs_layer), jnp.stack(outs_query), jnp.stack(outs_key), jnp.stack(outs_value), grad_weight)
```

```python
import jax
import jax.numpy as jnp
from jax import lax
from jax.experimental import pallas as pl
from jax.experimental.pallas import tpu as pltpu
from jax.sharding import PartitionSpec as P

HEADS = 16
HEAD_WIDTH = 48
ROWS = 256
WIDTH = 768
PEERS = 64
LANES = 128
SCALE = HEAD_WIDTH ** -0.5
MASKED = -1e30
BF = jnp.bfloat16
F32 = jnp.float32
SEND_ROWS = 40
BACK_ROWS = 56
PART_ROWS = 40


def iota(shape, dim):
    return lax.broadcasted_iota(jnp.int32, shape, dim)


def head_of(feature):
    return (feature * 1366) >> 16


def onehot(mask):
    return jnp.where(mask, 1.0, 0.0).astype(BF)


def nn(a, b):
    return lax.dot_general(a, b, (((1,), (0,)), ((), ())), preferred_element_type=F32)


def nt(a, b):
    return lax.dot_general(a, b, (((1,), (1,)), ((), ())), preferred_element_type=F32)


def tn(a, b):
    return lax.dot_general(a, b, (((0,), (0,)), ((), ())), preferred_element_type=F32)


def own_head_mask():
    return onehot(head_of(iota((ROWS, WIDTH), 1)) == (iota((ROWS, WIDTH), 0) & 15))


def fold(offset):
    f = iota((WIDTH, LANES), 0)
    lane = iota((WIDTH, LANES), 1) - offset
    return onehot((f - HEAD_WIDTH * head_of(f)) == lane)


def unfold(offset):
    f = iota((LANES, WIDTH), 1)
    lane = iota((LANES, WIDTH), 0) - offset
    return onehot((f - HEAD_WIDTH * head_of(f)) == lane)


def split3(x):
    hi = x.astype(BF).astype(F32)
    mid = (x - hi).astype(BF).astype(F32)
    return hi, mid, (x - hi - mid).astype(BF).astype(F32)


def pack_kernel(sc_ref, q_ref, k_ref, v_ref, g_ref, out_ref, scr):
    row_start, tile_count = sc_ref[0], sc_ref[1]
    own = own_head_mask()
    q_own = q_ref[...] * own
    valid_key = (row_start + iota((ROWS, ROWS), 1)) < tile_count
    s = jnp.where(valid_key, nt(q_own, k_ref[...]) * SCALE, MASKED)
    m = jnp.max(s, axis=1, keepdims=True)
    p = jnp.exp(s - m)
    l = jnp.sum(p, axis=1, keepdims=True)
    o = (nn(p.astype(BF), v_ref[...]) * (1.0 / l)).astype(BF) * own
    hi, mid, lo = split3(m + jnp.log(l))
    first, second = fold(0), fold(HEAD_WIDTH)
    lane = iota((ROWS, LANES), 1)
    d = nn(q_own, first) + nn(o, second)
    d = jnp.where(lane == 96, hi, jnp.where(lane == 97, mid, jnp.where(lane == 98, lo, d)))
    c = (nn(k_ref[...] * own, first) + nn(v_ref[...] * own, second)).astype(BF)
    r = iota((PEERS * 16, ROWS), 0)
    col = iota((PEERS * 16, ROWS), 1)
    x = nn(onehot(col == 16 * (r & 15) + (r >> 6)), c)
    mine = 16 * (4 * ((r >> 4) & 3) + (r & 3)) + (r >> 6)
    for a in range(4):
        part = d if a == 3 else pltpu.roll(d, 96 - 32 * a, 1)
        part = jnp.where(lane >= 96, part, 0.0).astype(BF)
        x = x + nn(onehot((col == mine) & (((r >> 2) & 3) == a)), part)
    out_ref[:, 0:16, :] = x.astype(BF).reshape(PEERS, 16, LANES)
    valid_row = (row_start + iota((ROWS, WIDTH), 0)) < tile_count
    g = jnp.where(valid_row, g_ref[...].astype(F32), 0.0).astype(BF)
    r2, c2 = iota((ROWS, ROWS), 0), iota((ROWS, ROWS), 1)
    gx = nn(onehot(c2 == 16 * (4 * (r2 & 3) + (r2 >> 6)) + ((r2 & 63) >> 2)), g)
    for t in range(6):
        for ii in range(4):
            scr[pl.ds(4 * t + ii, PEERS, stride=24), :] = gx[64 * ii : 64 * ii + 64, 128 * t : 128 * t + 128]
    out_ref[:, 16:40, :] = scr[...].reshape(PEERS, 24, LANES).astype(BF)


def near_kernel(sc_ref, q_ref, k_ref, v_ref, g_ref, w_ref, dq_ref, dk_ref, dv_ref, att_ref, ga_ref, keep_ref, send_ref,
                qt, kt, vt, gat, at, dqt, dkt, dvt, big, halves):
    row_start, tile_count, core = sc_ref[0], sc_ref[1], sc_ref[3]
    valid_row = (row_start + iota((ROWS, WIDTH), 0)) < tile_count
    g = jnp.where(valid_row, g_ref[...].astype(F32), 0.0).astype(BF)
    gat[...] = nt(w_ref[...], g).astype(BF)
    ga_ref[...] = nt(g, w_ref[...]).astype(BF)
    qt[...] = q_ref[...].T
    kt[...] = k_ref[...].T
    vt[...] = v_ref[...].T
    valid_key = (row_start + iota((ROWS, ROWS), 0)) < tile_count
    column = iota((1, ROWS), 1) & 15
    for h in range(HEADS):
        f = HEAD_WIDTH * h
        a, b = f // LANES * LANES, -(-(f + HEAD_WIDTH) // LANES) * LANES
        lane = a + iota((ROWS, b - a), 1)
        here = onehot((lane >= f) & (lane < f + HEAD_WIDTH))
        rows = slice(f, f + HEAD_WIDTH)
        s = jnp.where(valid_key, nn(k_ref[:, a:b] * here, qt[a:b, :]) * SCALE, MASKED)
        m = jnp.max(s, axis=0, keepdims=True)
        p = jnp.exp(s - m)
        l = jnp.sum(p, axis=0, keepdims=True)
        inv = jnp.where(column == h, 0.0, 1.0 / l)
        att = (nn(vt[rows, :], p.astype(BF)) * inv).astype(BF)
        at[rows, :] = att
        ga = gat[rows, :]
        delta = jnp.sum(ga.astype(F32) * att.astype(F32), axis=0, keepdims=True)
        dp = nn(v_ref[:, a:b] * here, gat[a:b, :])
        p = p * inv
        ds = (p * (dp - delta)).astype(BF)
        dqt[rows, :] = nn(kt[rows, :], ds) * SCALE
        dkt[rows, :] = nt(qt[rows, :], ds) * SCALE
        dvt[rows, :] = nt(ga, p.astype(BF))
    dq_ref[...] = dqt[...].T
    dk_ref[...] = dkt[...].T
    dv_ref[...] = dvt[...].T
    att_ref[...] = at[...].T
    partial = nn(at[...], g)
    for t in range(6):
        big[t] = partial[:, 128 * t : 128 * t + 128]
    zero = jnp.zeros((PEERS, LANES), F32)
    for c in range(2):
        for i in range(6):
            for t in range(6):
                piece = big[t, pl.ds(6 * c + i, PEERS, stride=12), :]
                halves[c, pl.ds(6 * i + t, PEERS, stride=PART_ROWS), :] = piece
        for i in range(36, PART_ROWS):
            halves[c, pl.ds(i, PEERS, stride=PART_ROWS), :] = zero
    first, second = halves[0], halves[1]
    shape = (PEERS, PART_ROWS, LANES)
    keep_ref[...] = jnp.where(core == 0, first, second).astype(BF).reshape(shape)
    send_ref[...] = jnp.where(core == 0, second, first).astype(BF).reshape(shape)


def far_kernel(sc_ref, x_ref, w_ref, keep_ref, got_ref, back_ref, skeep_ref, ssend_ref, xs, gs, ps, ss, so):
    tile_count, head, core = sc_ref[1], sc_ref[2], sc_ref[3]
    x = x_ref[:, 0:16, :].reshape(PEERS * 16, LANES)
    xs[...] = x.astype(F32)
    gs[...] = x_ref[:, 16:40, :].astype(F32).reshape(PEERS * 24, LANES)
    lane = iota((PEERS, LANES), 1)
    parts, grads = [], []
    for ii in range(4):
        total = jnp.zeros((PEERS, LANES), F32)
        for a in range(4):
            piece = xs[pl.ds(4 * a + ii, PEERS, stride=16), :]
            piece = piece if a == 3 else pltpu.roll(piece, 32 + 32 * a, 1)
            total = jnp.where((lane >> 5) == a, piece, total)
        parts.append(total)
        grads.append(jnp.concatenate([gs[pl.ds(4 * t + ii, PEERS, stride=24), :] for t in range(6)], axis=1))
    d = jnp.concatenate(parts, axis=0)
    g = jnp.concatenate(grads, axis=0).astype(BF)
    dt = d.T
    row = iota((LANES, ROWS), 0)
    q_t = jnp.where(row < 48, dt, 0.0).astype(BF)
    q_row = jnp.where(iota((ROWS, LANES), 1) < 48, d, 0.0).astype(BF)
    lse_near = jnp.sum(jnp.where((row >= 96) & (row < 99), dt, 0.0), axis=0, keepdims=True)
    valid_key = (16 * iota((PEERS * 16, ROWS), 0) + head) < tile_count
    s = jnp.where(valid_key, nn(x, q_t) * SCALE, MASKED)
    m = jnp.maximum(jnp.max(s, axis=0, keepdims=True), lse_near)
    p = jnp.exp(s - m)
    near = jnp.exp(lse_near - m)
    l = jnp.sum(p, axis=0, keepdims=True) + near
    inv = 1.0 / l
    xt = xs[...].T.astype(BF)
    middle = (row >= 48) & (row < 96)
    att = jnp.where(middle, (nn(xt, p.astype(BF)) + near * dt) * inv, 0.0).astype(BF)
    w_head = w_ref[pl.ds(pl.multiple_of(head * HEAD_WIDTH, 16), HEAD_WIDTH), :]
    w_pad = jnp.concatenate([jnp.zeros((48, WIDTH), BF), w_head, jnp.zeros((32, WIDTH), BF)], axis=0)
    ga_t = nt(w_pad, g)
    ga_row = ga_t.T.astype(BF)
    ga_t = ga_t.astype(BF)
    delta = jnp.sum(ga_t.astype(F32) * att.astype(F32), axis=0, keepdims=True)
    dp = nn(x, ga_t)
    p = p * inv
    ds = (p * (dp - delta)).astype(BF)
    dq = nn(xt, ds) * SCALE
    hi, mid, lo = split3(m + jnp.log(l))
    e = jnp.where(row < 48, dq, att.astype(F32))
    e = jnp.where(row == 96, hi, jnp.where(row == 97, mid, jnp.where(row == 98, lo, e)))
    e = e.T
    ps[...] = nn(ds, q_row) * SCALE + nn(p.astype(BF), ga_row)
    for ii in range(4):
        for a in range(4):
            piece = e[64 * ii : 64 * ii + 64, :]
            piece = piece if a == 3 else pltpu.roll(piece, 96 - 32 * a, 1)
            at = pl.ds(4 * a + ii, PEERS, stride=16)
            ps[at, :] = jnp.where(lane >= 96, piece, ps[at, :])
    back_ref[:, 0:16, :] = ps[...].astype(BF).reshape(PEERS, 16, LANES)
    back_ref[:, 16:56, :] = (keep_ref[...].astype(F32) + got_ref[...].astype(F32)).astype(BF)
    partial = nn(att, g)
    for t in range(6):
        ss[t] = partial[48:96, 128 * t : 128 * t + 128]
    zero = jnp.zeros((4, LANES), F32)
    for c in range(2):
        for i in range(6):
            for t in range(6):
                piece = ss[t, pl.ds(6 * c + i, 4, stride=12), :]
                so[c, pl.ds(6 * i + t, 4, stride=PART_ROWS), :] = piece
        for i in range(36, PART_ROWS):
            so[c, pl.ds(i, 4, stride=PART_ROWS), :] = zero
    first, second = so[0], so[1]
    shape = (4, PART_ROWS, LANES)
    skeep_ref[...] = jnp.where(core == 0, first, second).astype(BF).reshape(shape)
    ssend_ref[...] = jnp.where(core == 0, second, first).astype(BF).reshape(shape)


def add_kernel(sc_ref, back_ref, keep_ref, got_ref, out_ref):
    out_ref[:, 0:16, :] = back_ref[:, 0:16, :]
    extra = keep_ref[...].astype(F32) + got_ref[...].astype(F32)
    out_ref[:, 16:56, :] = (back_ref[:, 16:56, :].astype(F32) + extra).astype(BF)


def final_kernel(sc_ref, q_ref, k_ref, v_ref, w_ref, x_ref, dq0_ref, dk0_ref, dv0_ref, att0_ref, ga_ref,
                 out_ref, dq_ref, dk_ref, dv_ref):
    row_start, tile_count = sc_ref[0], sc_ref[1]
    x = x_ref[:, 0:16, :].reshape(PEERS * 16, LANES)
    row, col = iota((ROWS, PEERS * 16), 0), iota((ROWS, PEERS * 16), 1)
    lane = iota((ROWS, LANES), 1)
    dkv = nn(onehot(row == 16 * (col & 15) + (col >> 6)), x)
    dkv = jnp.where(lane < 96, dkv, 0.0).astype(BF)
    source = 64 * (row & 15) + 16 * (row >> 6) + ((row >> 4) & 3)
    e = jnp.zeros((ROWS, LANES), F32)
    for a in range(4):
        piece = nn(onehot(col == source + 4 * a), x)
        piece = piece if a == 3 else pltpu.roll(piece, 32 + 32 * a, 1)
        e = jnp.where((lane >> 5) == a, piece, e)
    lse = jnp.sum(jnp.where((lane >= 96) & (lane < 99), e, 0.0), axis=1, keepdims=True)
    e = jnp.where(lane < 96, e, 0.0).astype(BF)
    own = own_head_mask()
    own32 = own.astype(F32)
    first, second = unfold(0), unfold(HEAD_WIDTH)
    att = (att0_ref[...].astype(F32) + nn(e, second) * own32).astype(BF)
    valid_row = (row_start + iota((ROWS, WIDTH), 0)) < tile_count
    out_ref[...] = jnp.where(valid_row, nn(att, w_ref[...]), 0.0).astype(BF)
    q_own = q_ref[...] * own
    ga_own = ga_ref[...] * own
    valid_key = (row_start + iota((ROWS, ROWS), 1)) < tile_count
    s = jnp.where(valid_key, nt(q_own, k_ref[...]) * SCALE, MASKED)
    p = jnp.exp(s - lse)
    delta = jnp.sum(ga_own.astype(F32) * att.astype(F32), axis=1, keepdims=True)
    ds = (p * (nt(ga_own, v_ref[...]) - delta)).astype(BF)
    dq_ref[...] = (dq0_ref[...] + (nn(ds, k_ref[...]) * SCALE + nn(e, first)) * own32).astype(BF)
    dk_ref[...] = (dk0_ref[...] + tn(ds, q_own) * SCALE + nn(dkv, first) * own32).astype(BF)
    dv_ref[...] = (dv0_ref[...] + tn(p.astype(BF), ga_own) + nn(dkv, second) * own32).astype(BF)


def call(kernel, inputs, outs, scratch=()):
    vmem = pl.BlockSpec(memory_space=pltpu.VMEM)
    return pl.pallas_call(
        kernel,
        out_shape=[jax.ShapeDtypeStruct(s, t) for s, t in outs],
        in_specs=[pl.BlockSpec(memory_space=pltpu.SMEM)] + [vmem] * (len(inputs) - 1),
        out_specs=[vmem] * len(outs),
        scratch_shapes=list(scratch),
        compiler_params=pltpu.CompilerParams(vmem_limit_bytes=56 * 1024 * 1024),
    )(*inputs)


def on_device(query_rows, key_rows, value_rows, grad_out, out_weight, tile_counts):
    q, k, v, g = query_rows[0], key_rows[0], value_rows[0], grad_out[0]
    place = lax.axis_index("seq")
    core = lax.axis_index("slide") % 2
    sc = jnp.stack([place * ROWS, tile_counts[0], place // 4, core]).astype(jnp.int32)
    other_core = [(0, 1), (1, 0), (2, 3), (3, 2)]

    (send,) = call(pack_kernel, (sc, q, k, v, g), [((PEERS, SEND_ROWS, LANES), BF)], [pltpu.VMEM((PEERS * 24, LANES), F32)])
    x = lax.all_to_all(send, "seq", 0, 0)

    tall = lambda t: pltpu.VMEM((WIDTH, ROWS), t)
    flat = (ROWS, WIDTH)
    part = (PEERS, PART_ROWS, LANES)
    dq0, dk0, dv0, att0, ga, keep, swap = call(
        near_kernel,
        (sc, q, k, v, g, out_weight),
        [(flat, F32)] * 3 + [(flat, BF)] * 2 + [(part, BF)] * 2,
        [tall(BF)] * 5 + [tall(F32)] * 3 + [pltpu.VMEM((6, WIDTH, LANES), F32), pltpu.VMEM((2, PEERS * PART_ROWS, LANES), F32)],
    )
    got = lax.ppermute(swap, "slide", other_core)

    small = (4, PART_ROWS, LANES)
    back, skeep, sswap = call(
        far_kernel,
        (sc, x, out_weight, keep, got),
        [((PEERS, BACK_ROWS, LANES), BF), (small, BF), (small, BF)],
        [
            pltpu.VMEM((PEERS * 16, LANES), F32),
            pltpu.VMEM((PEERS * 24, LANES), F32),
            pltpu.VMEM((PEERS * 16, LANES), F32),
            pltpu.VMEM((6, HEAD_WIDTH, LANES), F32),
            pltpu.VMEM((2, 4 * PART_ROWS, LANES), F32),
        ],
    )
    sgot = lax.ppermute(sswap, "slide", other_core)
    block = pl.BlockSpec((4, BACK_ROWS, LANES), lambda i, s: (s[2], 0, 0))
    whole = pl.BlockSpec(small, lambda i, s: (0, 0, 0))
    back = pl.pallas_call(
        add_kernel,
        out_shape=jax.ShapeDtypeStruct((PEERS, BACK_ROWS, LANES), BF),
        grid_spec=pltpu.PrefetchScalarGridSpec(
            num_scalar_prefetch=1, grid=(1,), in_specs=[block, whole, whole], out_specs=block
        ),
        input_output_aliases={1: 0},
    )(sc, back, skeep, sgot)
    y = lax.all_to_all(back, "seq", 0, 0)

    weight = jnp.sum(y[:, 16:56, :].astype(F32), axis=0)
    weight = lax.all_gather(weight, "slide")
    weight = (weight[0:2] + weight[2:4])[:, 0:36].reshape(12, WIDTH)

    outs = call(
        final_kernel, (sc, q, k, v, out_weight, y, dq0, dk0, dv0, att0, ga), [(flat, BF)] * 4
    )
    return tuple(o[None] for o in outs) + (weight,)


def solution(mesh):
    rows = P("slide", "seq", None)
    return jax.shard_map(
        on_device,
        mesh=mesh,
        in_specs=(rows, rows, rows, rows, P(), P("slide")),
        out_specs=(rows, rows, rows, rows, P("seq", None)),
        check_vma=False,
    )
```

```python
import jax
import jax.numpy as jnp
from jax import lax
from jax.experimental import pallas as pl
from jax.experimental.pallas import tpu as pltpu
from jax.sharding import PartitionSpec as P

HEADS = 16
HEAD_WIDTH = 48
ROWS = 256
WIDTH = 768
PEERS = 64
LANES = 128
SCALE = HEAD_WIDTH ** -0.5
MASKED = -1e30
BF = jnp.bfloat16
F32 = jnp.float32
SEND_ROWS = 40
BACK_ROWS = 56
PART_ROWS = 40


def iota(shape, dim):
    return lax.broadcasted_iota(jnp.int32, shape, dim)


def head_of(feature):
    return (feature * 1366) >> 16


def onehot(mask):
    return jnp.where(mask, 1.0, 0.0).astype(BF)


def nn(a, b):
    return lax.dot_general(a, b, (((1,), (0,)), ((), ())), preferred_element_type=F32)


def nt(a, b):
    return lax.dot_general(a, b, (((1,), (1,)), ((), ())), preferred_element_type=F32)


def tn(a, b):
    return lax.dot_general(a, b, (((0,), (0,)), ((), ())), preferred_element_type=F32)


def own_head_mask():
    return onehot(head_of(iota((ROWS, WIDTH), 1)) == (iota((ROWS, WIDTH), 0) & 15))


def fold(offset):
    f = iota((WIDTH, LANES), 0)
    lane = iota((WIDTH, LANES), 1) - offset
    return onehot((f - HEAD_WIDTH * head_of(f)) == lane)


def unfold(offset):
    f = iota((LANES, WIDTH), 1)
    lane = iota((LANES, WIDTH), 0) - offset
    return onehot((f - HEAD_WIDTH * head_of(f)) == lane)


def split3(x):
    hi = x.astype(BF).astype(F32)
    mid = (x - hi).astype(BF).astype(F32)
    return hi, mid, (x - hi - mid).astype(BF).astype(F32)


def pack_kernel(sc_ref, q_ref, k_ref, v_ref, g_ref, out_ref, next_ref, rows, grads):
    for n in range(5):
        next_ref[n] = sc_ref[n]
    row_start, tile_count = sc_ref[0], sc_ref[1]
    own = own_head_mask()
    q_own = q_ref[...] * own
    valid_key = (row_start + iota((ROWS, ROWS), 1)) < tile_count
    s = jnp.where(valid_key, nt(q_own, k_ref[...]) * SCALE, MASKED)
    m = jnp.max(s, axis=1, keepdims=True)
    p = jnp.exp(s - m)
    l = jnp.sum(p, axis=1, keepdims=True)
    o = (nn(p.astype(BF), v_ref[...]) * (1.0 / l)).astype(BF) * own
    hi, mid, lo = split3(m + jnp.log(l))
    first, second = fold(0), fold(HEAD_WIDTH)
    lane = iota((ROWS, LANES), 1)
    d = nn(q_own, first) + nn(o, second)
    d = jnp.where(lane == 96, hi, jnp.where(lane == 97, mid, jnp.where(lane == 98, lo, d)))
    c = nn(k_ref[...] * own, first) + nn(v_ref[...] * own, second)
    late = iota((16, LANES), 1) >= 96
    for a in range(4):
        turned = d if a == 3 else pltpu.roll(d, 96 - 32 * a, 1)
        for ii in range(4):
            i = 4 * a + ii
            for j in range(4):
                at = 16 * (4 * j + ii)
                rows[pl.ds(16 * j + i, 16, stride=64), :] = jnp.where(late, turned[at : at + 16], c[16 * i : 16 * i + 16])
    out_ref[:, 0:16, :] = rows[...].astype(BF).reshape(PEERS, 16, LANES)
    valid_row = (row_start + iota((ROWS, WIDTH), 0)) < tile_count
    g = jnp.where(valid_row, g_ref[...].astype(F32), 0.0)
    for j in range(4):
        for ii in range(4):
            at = 16 * (4 * j + ii)
            for t in range(6):
                grads[pl.ds(24 * j + 4 * t + ii, 16, stride=96), :] = g[at : at + 16, 128 * t : 128 * t + 128]
    out_ref[:, 16:40, :] = grads[...].astype(BF).reshape(PEERS, 24, LANES)


def head_window(h):
    f = HEAD_WIDTH * h
    a, b = f // LANES * LANES, -(-(f + HEAD_WIDTH) // LANES) * LANES
    lane = a + iota((ROWS, b - a), 1)
    return slice(a, b), slice(f, f + HEAD_WIDTH), onehot((lane >= f) & (lane < f + HEAD_WIDTH))


def forward_kernel(sc_ref, q_ref, k_ref, v_ref, g_ref, at_ref, lse_ref, keep_ref, send_ref, qt, vt, big, part):
    row_start, tile_count, core = sc_ref[0], sc_ref[1], sc_ref[3]
    valid_row = (row_start + iota((ROWS, WIDTH), 0)) < tile_count
    g = jnp.where(valid_row, g_ref[...].astype(F32), 0.0).astype(BF)
    qt[...] = q_ref[...].T
    vt[...] = v_ref[...].T
    valid_key = (row_start + iota((ROWS, ROWS), 0)) < tile_count
    column = iota((1, ROWS), 1) & 15
    for h in range(HEADS):
        window, rows, here = head_window(h)
        s = jnp.where(valid_key, nn(k_ref[:, window] * here, qt[window, :]) * SCALE, MASKED)
        m = jnp.max(s, axis=0, keepdims=True)
        p = jnp.exp(s - m)
        l = jnp.sum(p, axis=0, keepdims=True)
        inv = jnp.where(column == h, 0.0, 1.0 / l)
        at_ref[rows, :] = (nn(vt[rows, :], p.astype(BF)) * inv).astype(BF)
        lse_ref[h : h + 1, :] = jnp.where(column == h, 1e30, m + jnp.log(l))
    partial = nn(at_ref[...], g)
    for t in range(6):
        big[t] = partial[:, 128 * t : 128 * t + 128]
    zero = jnp.zeros((PEERS, LANES), F32)
    for i in range(36, PART_ROWS):
        part[pl.ds(i, PEERS, stride=PART_ROWS), :] = zero
    for ref, c in ((keep_ref, core), (send_ref, 1 - core)):
        for i in range(6):
            for t in range(6):
                part[pl.ds(6 * i + t, PEERS, stride=PART_ROWS), :] = big[t, pl.ds(6 * c + i, PEERS, stride=12), :]
        ref[...] = part[...].astype(BF).reshape(PEERS, PART_ROWS, LANES)


def join_kernel(sc_ref, keep_ref, got_ref, out_ref):
    out_ref[:, 0:16, :] = jnp.zeros((PEERS, 16, LANES), BF)
    out_ref[:, 16:56, :] = (keep_ref[...].astype(F32) + got_ref[...].astype(F32)).astype(BF)


def backward_kernel(sc_ref, q_ref, k_ref, v_ref, g_ref, w_ref, at_ref, lse_ref, strided_ref,
                    dq_ref, dk_ref, dv_ref, layer_ref, ga_ref, s_ref, dp_ref, pass_ref, qt, kt, gat, dqt, dkt, dvt):
    row_start, tile_count = sc_ref[0], sc_ref[1]
    pass_ref[...] = strided_ref[...]
    valid_row = (row_start + iota((ROWS, WIDTH), 0)) < tile_count
    g = jnp.where(valid_row, g_ref[...].astype(F32), 0.0).astype(BF)
    gat[...] = nt(w_ref[...], g).astype(BF)
    ga_row = nt(g, w_ref[...]).astype(BF)
    qt[...] = q_ref[...].T
    kt[...] = k_ref[...].T
    valid_key = (row_start + iota((ROWS, ROWS), 0)) < tile_count
    for h in range(HEADS):
        window, rows, here = head_window(h)
        s = jnp.where(valid_key, nn(k_ref[:, window] * here, qt[window, :]) * SCALE, MASKED)
        p = jnp.exp(s - lse_ref[h : h + 1, :])
        ga = gat[rows, :]
        delta = jnp.sum(ga.astype(F32) * at_ref[rows, :].astype(F32), axis=0, keepdims=True)
        dp = nn(v_ref[:, window] * here, gat[window, :])
        ds = (p * (dp - delta)).astype(BF)
        dqt[rows, :] = nn(kt[rows, :], ds) * SCALE
        dkt[rows, :] = nt(qt[rows, :], ds) * SCALE
        dvt[rows, :] = nt(ga, p.astype(BF))
    dq_ref[...] = dqt[...].T
    dk_ref[...] = dkt[...].T
    dv_ref[...] = dvt[...].T
    own = own_head_mask()
    ga_own = ga_row * own
    ga_ref[...] = ga_own
    layer_ref[...] = nn(at_ref[...].T, w_ref[...])
    valid_key = (row_start + iota((ROWS, ROWS), 1)) < tile_count
    s_ref[...] = jnp.where(valid_key, nt(q_ref[...] * own, k_ref[...]) * SCALE, MASKED)
    dp_ref[...] = nt(ga_own, v_ref[...])


def far_kernel(sc_ref, x_ref, w_ref, joined_ref, back_ref, strided_ref, xs, gs, ps):
    tile_count, head = sc_ref[1], sc_ref[2]
    x = x_ref[:, 0:16, :].reshape(PEERS * 16, LANES)
    xs[...] = x.astype(F32)
    gs[...] = x_ref[:, 16:40, :].astype(F32).reshape(PEERS * 24, LANES)
    lane = iota((PEERS, LANES), 1)
    parts, grads = [], []
    for ii in range(4):
        total = jnp.zeros((PEERS, LANES), F32)
        for a in range(4):
            piece = xs[pl.ds(4 * a + ii, PEERS, stride=16), :]
            piece = piece if a == 3 else pltpu.roll(piece, 32 + 32 * a, 1)
            total = jnp.where((lane >> 5) == a, piece, total)
        parts.append(total)
        grads.append(jnp.concatenate([gs[pl.ds(4 * t + ii, PEERS, stride=24), :] for t in range(6)], axis=1))
    d = jnp.concatenate(parts, axis=0)
    g = jnp.concatenate(grads, axis=0).astype(BF)
    dt = d.T
    row = iota((LANES, ROWS), 0)
    q_t = jnp.where(row < 48, dt, 0.0).astype(BF)
    q_row = jnp.where(iota((ROWS, LANES), 1) < 48, d, 0.0).astype(BF)
    lse_near = jnp.sum(jnp.where((row >= 96) & (row < 99), dt, 0.0), axis=0, keepdims=True)
    valid_key = (16 * iota((PEERS * 16, ROWS), 0) + head) < tile_count
    s = jnp.where(valid_key, nn(x, q_t) * SCALE, MASKED)
    m = jnp.maximum(jnp.max(s, axis=0, keepdims=True), lse_near)
    p = jnp.exp(s - m)
    near = jnp.exp(lse_near - m)
    l = jnp.sum(p, axis=0, keepdims=True) + near
    inv = 1.0 / l
    xt = xs[...].T.astype(BF)
    middle = (row >= 48) & (row < 96)
    att = jnp.where(middle, (nn(xt, p.astype(BF)) + near * dt) * inv, 0.0).astype(BF)
    w_pad = jnp.concatenate([jnp.zeros((48, WIDTH), BF), w_ref[...], jnp.zeros((32, WIDTH), BF)], axis=0)
    ga_t = nt(w_pad, g)
    ga_row = ga_t.T.astype(BF)
    ga_t = ga_t.astype(BF)
    delta = jnp.sum(ga_t.astype(F32) * att.astype(F32), axis=0, keepdims=True)
    dp = nn(x, ga_t)
    p = p * inv
    ds = (p * (dp - delta)).astype(BF)
    dq = nn(xt, ds) * SCALE
    hi, mid, lo = split3(m + jnp.log(l))
    e = jnp.where(row < 48, dq, att.astype(F32))
    e = jnp.where(row == 96, hi, jnp.where(row == 97, mid, jnp.where(row == 98, lo, e)))
    e = e.T
    ps[...] = nn(ds, q_row) * SCALE + nn(p.astype(BF), ga_row)
    for a in range(4):
        turned = e if a == 3 else pltpu.roll(e, 96 - 32 * a, 1)
        for ii in range(4):
            at = pl.ds(4 * a + ii, PEERS, stride=16)
            ps[at, :] = jnp.where(lane >= 96, turned[64 * ii : 64 * ii + 64], ps[at, :])
    back_ref[...] = ps[...].astype(BF).reshape(PEERS, 16, LANES)
    partial = nn(att, g)
    for j in range(4):
        strided_ref[j] = partial[48 + 12 * j : 60 + 12 * j]


def final_kernel(sc_ref, q_ref, k_ref, w_ref, x_ref, s_ref, dp_ref, ga_ref, layer_ref, dq0_ref, dk0_ref, dv0_ref,
                 out_ref, dq_ref, dk_ref, dv_ref, xs):
    row_start, tile_count = sc_ref[0], sc_ref[1]
    xs[...] = x_ref[:, 0:16, :].astype(F32).reshape(PEERS * 16, LANES)
    lane = iota((16, LANES), 1)
    e_rows = [None] * 16
    dkv_rows = []
    for i in range(16):
        a, ii = i // 4, i % 4
        total = None
        for j in range(4):
            piece = xs[pl.ds(16 * j + i, 16, stride=64), :]
            total = piece if total is None else total + piece
            moved = piece if a == 3 else pltpu.roll(piece, 32 + 32 * a, 1)
            old = e_rows[4 * j + ii]
            e_rows[4 * j + ii] = moved if old is None else jnp.where((lane >> 5) == a, moved, old)
        dkv_rows.append(total)
    dkv = jnp.concatenate(dkv_rows, axis=0)
    e = jnp.concatenate(e_rows, axis=0)
    lane = iota((ROWS, LANES), 1)
    dkv = jnp.where(lane < 96, dkv, 0.0).astype(BF)
    lse = jnp.sum(jnp.where((lane >= 96) & (lane < 99), e, 0.0), axis=1, keepdims=True)
    e = jnp.where(lane < 96, e, 0.0).astype(BF)
    own = own_head_mask()
    own32 = own.astype(F32)
    first, second = unfold(0), unfold(HEAD_WIDTH)
    att = nn(e, second).astype(BF) * own
    valid_row = (row_start + iota((ROWS, WIDTH), 0)) < tile_count
    out_ref[...] = jnp.where(valid_row, layer_ref[...] + nn(att, w_ref[...]), 0.0).astype(BF)
    q_own = q_ref[...] * own
    ga_own = ga_ref[...]
    p = jnp.exp(s_ref[...] - lse)
    delta = jnp.sum(ga_own.astype(F32) * att.astype(F32), axis=1, keepdims=True)
    ds = (p * (dp_ref[...] - delta)).astype(BF)
    dq_ref[...] = (dq0_ref[...] + (nn(ds, k_ref[...]) * SCALE + nn(e, first)) * own32).astype(BF)
    dk_ref[...] = (dk0_ref[...] + tn(ds, q_own) * SCALE + nn(dkv, first) * own32).astype(BF)
    dv_ref[...] = (dv0_ref[...] + tn(p.astype(BF), ga_own) + nn(dkv, second) * own32).astype(BF)


def call(kernel, inputs, outs, scratch=(), scalars=False):
    vmem = pl.BlockSpec(memory_space=pltpu.VMEM)
    smem = pl.BlockSpec(memory_space=pltpu.SMEM)
    return pl.pallas_call(
        kernel,
        out_shape=[jax.ShapeDtypeStruct(s, t) for s, t in outs],
        in_specs=[smem] + [vmem] * (len(inputs) - 1),
        out_specs=[vmem] * (len(outs) - 1) + [smem if scalars else vmem],
        scratch_shapes=[pltpu.VMEM(s, t) for s, t in scratch],
        compiler_params=pltpu.CompilerParams(vmem_limit_bytes=56 * 1024 * 1024),
    )(*inputs)


def on_device(query_rows, key_rows, value_rows, grad_out, out_weight, tile_counts):
    q, k, v, g = query_rows[0], key_rows[0], value_rows[0], grad_out[0]
    place = lax.axis_index("seq")
    slide = lax.axis_index("slide")
    core, far_x = slide % 2, slide // 2
    sc = jnp.stack([place * ROWS, tile_counts[0], place // 4, core, far_x]).astype(jnp.int32)
    other_core = [(0, 1), (1, 0), (2, 3), (3, 2)]
    other_x = [(0, 2), (2, 0), (1, 3), (3, 1)]
    flat, tall = (ROWS, WIDTH), (WIDTH, ROWS)

    send, sc2 = call(
        pack_kernel, (sc, q, k, v, g), [((PEERS, SEND_ROWS, LANES), BF), ((5,), jnp.int32)],
        [((PEERS * 16, LANES), F32), ((PEERS * 24, LANES), F32)], scalars=True,
    )
    x = lax.all_to_all(send, "seq", 0, 0)

    part = (PEERS, PART_ROWS, LANES)
    at0, lse0, keep, swap = call(
        forward_kernel, (sc2, q, k, v, g), [(tall, BF), ((HEADS, ROWS), F32), (part, BF), (part, BF)],
        [(tall, BF), (tall, BF), ((6, WIDTH, LANES), F32), ((PEERS * PART_ROWS, LANES), F32)],
    )
    got = lax.ppermute(swap, "slide", other_core)
    (joined,) = call(join_kernel, (sc2, keep, got), [((PEERS, BACK_ROWS, LANES), BF)])

    w_head = lax.dynamic_slice_in_dim(out_weight, place // 4 * HEAD_WIDTH, HEAD_WIDTH, 0)
    whole = lambda *shape: pl.BlockSpec(shape, lambda i: (0,) * len(shape))
    back, strided = pl.pallas_call(
        far_kernel,
        grid=(1,),
        out_shape=[jax.ShapeDtypeStruct((PEERS, BACK_ROWS, LANES), BF), jax.ShapeDtypeStruct((4, 12, WIDTH), F32)],
        in_specs=[
            pl.BlockSpec(memory_space=pltpu.SMEM),
            whole(PEERS, SEND_ROWS, LANES),
            whole(HEAD_WIDTH, WIDTH),
            pl.BlockSpec(memory_space=pl.ANY),
        ],
        out_specs=[whole(PEERS, 16, LANES), whole(4, 12, WIDTH)],
        scratch_shapes=[pltpu.VMEM((PEERS * n, LANES), F32) for n in (16, 24, 16)],
        input_output_aliases={3: 0},
        compiler_params=pltpu.CompilerParams(vmem_limit_bytes=56 * 1024 * 1024),
    )(sc, x, w_head, joined)
    y = lax.all_to_all(back, "seq", 0, 0)

    dq0, dk0, dv0, layer0, ga, s0, dp0, strided = call(
        backward_kernel, (sc, q, k, v, g, out_weight, at0, lse0, strided),
        [(flat, F32)] * 4 + [(flat, BF)] + [((ROWS, ROWS), F32)] * 2 + [((4, 12, WIDTH), F32)],
        [(tall, BF)] * 3 + [(tall, F32)] * 3,
    )
    rest = jnp.sum(y[:, 16:52, :].astype(F32), axis=0).reshape(6, WIDTH)
    weight = lax.dynamic_update_slice_in_dim(jnp.zeros((12, WIDTH), F32), rest, 6 * core, 0)
    quarter = place % 4
    for step in range(4):
        mine = lax.dynamic_index_in_dim(strided, (quarter + step) % 4, 0, keepdims=False)
        if step:
            ring = [(d, d // 4 * 4 + (d + step) % 4) for d in range(PEERS)]
            mine = lax.ppermute(mine, "seq", ring)
        weight = weight + mine
    weight = weight + sum(lax.ppermute(weight, "slide", [(n, n ^ bits) for n in range(4)]) for bits in (2, 3, 1))

    outs = call(
        final_kernel, (sc, q, k, out_weight, y, s0, dp0, ga, layer0, dq0, dk0, dv0), [(flat, BF)] * 4,
        [((PEERS * 16, LANES), F32)],
    )
    return tuple(o[None] for o in outs) + (weight,)


def solution(mesh):
    rows = P("slide", "seq", None)
    return jax.shard_map(
        on_device,
        mesh=mesh,
        in_specs=(rows, rows, rows, rows, P(), P("slide")),
        out_specs=(rows, rows, rows, rows, P("seq", None)),
        check_vma=False,
    )
```

```python
import jax
import jax.numpy as jnp
from jax import lax
from jax.experimental import pallas as pl
from jax.experimental.pallas import tpu as pltpu
from jax.sharding import PartitionSpec as P

HEADS = 16
HEAD_WIDTH = 48
ROWS = 256
WIDTH = 768
PEERS = 64
LANES = 128
SCALE = HEAD_WIDTH ** -0.5
MASKED = -1e30
BF = jnp.bfloat16
F32 = jnp.float32
SEND_ROWS = 40
BACK_ROWS = 56
PART_ROWS = 40
LIMIT = 48
GROUP = 4
POWER = SCALE * 1.4426950408889634


def iota(shape, dim):
    return lax.broadcasted_iota(jnp.int32, shape, dim)


def head_of(feature):
    return (feature * 1366) >> 16


def onehot(mask):
    return jnp.where(mask, 1.0, 0.0).astype(BF)


def nn(a, b):
    return lax.dot_general(a, b, (((1,), (0,)), ((), ())), preferred_element_type=F32)


def nt(a, b):
    return lax.dot_general(a, b, (((1,), (1,)), ((), ())), preferred_element_type=F32)


def tn(a, b):
    return lax.dot_general(a, b, (((0,), (0,)), ((), ())), preferred_element_type=F32)


def own_head_mask():
    return onehot(head_of(iota((ROWS, WIDTH), 1)) == (iota((ROWS, WIDTH), 0) & 15))


def fold(offset):
    f = iota((WIDTH, LANES), 0)
    lane = iota((WIDTH, LANES), 1) - offset
    return onehot((f - HEAD_WIDTH * head_of(f)) == lane)


def unfold(offset):
    f = iota((LANES, WIDTH), 1)
    lane = iota((LANES, WIDTH), 0) - offset
    return onehot((f - HEAD_WIDTH * head_of(f)) == lane)


def split3(x):
    hi = x.astype(BF).astype(F32)
    mid = (x - hi).astype(BF).astype(F32)
    return hi, mid, (x - hi - mid).astype(BF).astype(F32)


def pack_kernel(count_ref, q_ref, k_ref, v_ref, g_ref, out_ref, next_ref, rows, grads):
    place, slide = lax.axis_index("seq"), lax.axis_index("slide")
    row_start, tile_count = place * ROWS, count_ref[0]
    for n, value in enumerate((row_start, tile_count, place // 4, slide % 2, slide // 2)):
        next_ref[n] = value
    own = own_head_mask()
    q_own = q_ref[...] * own
    valid_key = (row_start + iota((ROWS, ROWS), 1)) < tile_count
    s = jnp.where(valid_key, nt(q_own, k_ref[...]) * SCALE, MASKED)
    m = jnp.max(s, axis=1, keepdims=True)
    p = jnp.exp(s - m)
    l = jnp.sum(p, axis=1, keepdims=True)
    o = (nn(p.astype(BF), v_ref[...]) * (1.0 / l)).astype(BF) * own
    hi, mid, lo = split3(m + jnp.log(l))
    first, second = fold(0), fold(HEAD_WIDTH)
    lane = iota((ROWS, LANES), 1)
    d = nn(q_own, first) + nn(o, second)
    d = jnp.where(lane == 96, hi, jnp.where(lane == 97, mid, jnp.where(lane == 98, lo, d)))
    c = nn(k_ref[...] * own, first) + nn(v_ref[...] * own, second)
    late = iota((16, LANES), 1) >= 96
    for a in range(4):
        turned = d if a == 3 else pltpu.roll(d, 96 - 32 * a, 1)
        for ii in range(4):
            i = 4 * a + ii
            for j in range(4):
                at = 16 * (4 * j + ii)
                rows[pl.ds(16 * j + i, 16, stride=64), :] = jnp.where(late, turned[at : at + 16], c[16 * i : 16 * i + 16])
    out_ref[:, 0:16, :] = rows[...].astype(BF).reshape(PEERS, 16, LANES)
    valid_row = (row_start + iota((ROWS, WIDTH), 0)) < tile_count
    g = jnp.where(valid_row, g_ref[...].astype(F32), 0.0)
    for j in range(4):
        for ii in range(4):
            at = 16 * (4 * j + ii)
            for t in range(6):
                grads[pl.ds(24 * j + 4 * t + ii, 16, stride=96), :] = g[at : at + 16, 128 * t : 128 * t + 128]
    out_ref[:, 16:40, :] = grads[...].astype(BF).reshape(PEERS, 24, LANES)


def head_window(h):
    f = HEAD_WIDTH * h
    a, b = f // LANES * LANES, -(-(f + HEAD_WIDTH) // LANES) * LANES
    lane = a + iota((ROWS, b - a), 1)
    return slice(a, b), slice(f, f + HEAD_WIDTH), onehot((lane >= f) & (lane < f + HEAD_WIDTH))


def forward_kernel(sc_ref, q_ref, k_ref, v_ref, g_ref, at_ref, lse_ref, keep_ref, send_ref, qt, vt, big, part):
    row_start, tile_count, core = sc_ref[0], sc_ref[1], sc_ref[3]
    valid_row = (row_start + iota((ROWS, WIDTH), 0)) < tile_count
    g = jnp.where(valid_row, g_ref[...].astype(F32), 0.0).astype(BF)
    qt[...] = q_ref[...].T
    vt[...] = v_ref[...].T
    valid_key = (row_start + iota((ROWS, ROWS), 0)) < tile_count
    column = iota((1, ROWS), 1) & 15
    for start in range(0, HEADS, GROUP):
        group = [(h, *head_window(h)) for h in range(start, start + GROUP)]
        scores = [jnp.where(valid_key, nn(k_ref[:, w] * here, qt[w, :]), MASKED) for _, w, _, here in group]
        tops = [jnp.max(s, axis=0, keepdims=True) * POWER for s in scores]
        probs = [jnp.exp2(s * POWER - m) for s, m in zip(scores, tops)]
        totals = [jnp.sum(p, axis=0, keepdims=True) for p in probs]
        sums = [nn(vt[rows, :], p.astype(BF)) for (_, _, rows, _), p in zip(group, probs)]
        for (h, _, rows, _), o, m, l in zip(group, sums, tops, totals):
            at_ref[rows, :] = (o * jnp.where(column == h, 0.0, 1.0 / l)).astype(BF)
            lse_ref[h : h + 1, :] = jnp.where(column == h, 1e30, m + jnp.log2(l))
    partial = nn(at_ref[...], g)
    for t in range(6):
        big[t] = partial[:, 128 * t : 128 * t + 128]
    zero = jnp.zeros((PEERS, LANES), F32)
    for i in range(36, PART_ROWS):
        part[pl.ds(i, PEERS, stride=PART_ROWS), :] = zero
    for ref, c in ((keep_ref, core), (send_ref, 1 - core)):
        for i in range(6):
            for t in range(6):
                part[pl.ds(6 * i + t, PEERS, stride=PART_ROWS), :] = big[t, pl.ds(6 * c + i, PEERS, stride=12), :]
        ref[...] = part[...].astype(BF).reshape(PEERS, PART_ROWS, LANES)


def join_kernel(sc_ref, keep_ref, got_ref, out_ref):
    out_ref[:, 0:16, :] = jnp.zeros((PEERS, 16, LANES), BF)
    out_ref[:, 16:56, :] = (keep_ref[...].astype(F32) + got_ref[...].astype(F32)).astype(BF)


def backward_kernel(sc_ref, q_ref, k_ref, v_ref, g_ref, w_ref, at_ref, lse_ref, strided_ref,
                    dq_ref, dk_ref, dv_ref, layer_ref, ga_ref, s_ref, dp_ref, pass_ref, qt, kt, gat, dqt, dkt, dvt):
    row_start, tile_count = sc_ref[0], sc_ref[1]
    pass_ref[...] = strided_ref[...]
    valid_row = (row_start + iota((ROWS, WIDTH), 0)) < tile_count
    g = jnp.where(valid_row, g_ref[...].astype(F32), 0.0).astype(BF)
    gat[...] = nt(w_ref[...], g).astype(BF)
    ga_row = nt(g, w_ref[...]).astype(BF)
    qt[...] = q_ref[...].T
    kt[...] = k_ref[...].T
    valid_key = (row_start + iota((ROWS, ROWS), 0)) < tile_count
    for start in range(0, HEADS, GROUP):
        group = [(h, *head_window(h)) for h in range(start, start + GROUP)]
        scores = [jnp.where(valid_key, nn(k_ref[:, w] * here, qt[w, :]), MASKED) for _, w, _, here in group]
        slopes = [nn(v_ref[:, w] * here, gat[w, :]) for _, w, _, here in group]
        probs = [jnp.exp2(s * POWER - lse_ref[h : h + 1, :]) for (h, _, _, _), s in zip(group, scores)]
        deltas = [
            jnp.sum(gat[rows, :].astype(F32) * at_ref[rows, :].astype(F32), axis=0, keepdims=True)
            for _, _, rows, _ in group
        ]
        steps = [(p * (dp - delta)).astype(BF) for p, dp, delta in zip(probs, slopes, deltas)]
        for (_, _, rows, _), p, ds in zip(group, probs, steps):
            dqt[rows, :] = nn(kt[rows, :], ds) * SCALE
            dkt[rows, :] = nt(qt[rows, :], ds) * SCALE
            dvt[rows, :] = nt(gat[rows, :], p.astype(BF))
    dq_ref[...] = dqt[...].T
    dk_ref[...] = dkt[...].T
    dv_ref[...] = dvt[...].T
    own = own_head_mask()
    ga_own = ga_row * own
    ga_ref[...] = ga_own
    layer_ref[...] = nn(at_ref[...].T, w_ref[...])
    valid_key = (row_start + iota((ROWS, ROWS), 1)) < tile_count
    s_ref[...] = jnp.where(valid_key, nt(q_ref[...] * own, k_ref[...]) * SCALE, MASKED)
    dp_ref[...] = nt(ga_own, v_ref[...])


def far_kernel(sc_ref, x_ref, w_ref, joined_ref, back_ref, strided_ref, xs, gs, ps):
    tile_count, head = sc_ref[1], sc_ref[2]
    x = x_ref[:, 0:16, :].reshape(PEERS * 16, LANES)
    xs[...] = x.astype(F32)
    gs[...] = x_ref[:, 16:40, :].astype(F32).reshape(PEERS * 24, LANES)
    lane = iota((PEERS, LANES), 1)
    parts, grads = [], []
    for ii in range(4):
        total = jnp.zeros((PEERS, LANES), F32)
        for a in range(4):
            piece = xs[pl.ds(4 * a + ii, PEERS, stride=16), :]
            piece = piece if a == 3 else pltpu.roll(piece, 32 + 32 * a, 1)
            total = jnp.where((lane >> 5) == a, piece, total)
        parts.append(total)
        grads.append(jnp.concatenate([gs[pl.ds(4 * t + ii, PEERS, stride=24), :] for t in range(6)], axis=1))
    d = jnp.concatenate(parts, axis=0)
    g = jnp.concatenate(grads, axis=0).astype(BF)
    dt = d.T
    row = iota((LANES, ROWS), 0)
    q_t = jnp.where(row < 48, dt, 0.0).astype(BF)
    q_row = jnp.where(iota((ROWS, LANES), 1) < 48, d, 0.0).astype(BF)
    lse_near = jnp.sum(jnp.where((row >= 96) & (row < 99), dt, 0.0), axis=0, keepdims=True)
    valid_key = (16 * iota((PEERS * 16, ROWS), 0) + head) < tile_count
    s = jnp.where(valid_key, nn(x, q_t) * SCALE, MASKED)
    m = jnp.maximum(jnp.max(s, axis=0, keepdims=True), lse_near)
    p = jnp.exp(s - m)
    near = jnp.exp(lse_near - m)
    l = jnp.sum(p, axis=0, keepdims=True) + near
    inv = 1.0 / l
    xt = xs[...].T.astype(BF)
    middle = (row >= 48) & (row < 96)
    att = jnp.where(middle, (nn(xt, p.astype(BF)) + near * dt) * inv, 0.0).astype(BF)
    w_pad = jnp.concatenate([jnp.zeros((48, WIDTH), BF), w_ref[...], jnp.zeros((32, WIDTH), BF)], axis=0)
    ga_t = nt(w_pad, g)
    ga_row = ga_t.T.astype(BF)
    ga_t = ga_t.astype(BF)
    delta = jnp.sum(ga_t.astype(F32) * att.astype(F32), axis=0, keepdims=True)
    dp = nn(x, ga_t)
    p = p * inv
    ds = (p * (dp - delta)).astype(BF)
    dq = nn(xt, ds) * SCALE
    hi, mid, lo = split3(m + jnp.log(l))
    e = jnp.where(row < 48, dq, att.astype(F32))
    e = jnp.where(row == 96, hi, jnp.where(row == 97, mid, jnp.where(row == 98, lo, e)))
    e = e.T
    ps[...] = nn(ds, q_row) * SCALE + nn(p.astype(BF), ga_row)
    for a in range(4):
        turned = e if a == 3 else pltpu.roll(e, 96 - 32 * a, 1)
        for ii in range(4):
            at = pl.ds(4 * a + ii, PEERS, stride=16)
            ps[at, :] = jnp.where(lane >= 96, turned[64 * ii : 64 * ii + 64], ps[at, :])
    back_ref[...] = ps[...].astype(BF).reshape(PEERS, 16, LANES)
    partial = nn(att, g)
    for j in range(4):
        strided_ref[j] = partial[48 + 12 * j : 60 + 12 * j]


def weight_kernel(sc_ref, y_ref, a_ref, b_ref, c_ref, d_ref, out_ref, scr):
    core = sc_ref[3]
    scr[...] = jnp.sum(y_ref[:, 16:56, :].astype(F32), axis=0)
    rest = jnp.concatenate([scr[pl.ds(t, 6, stride=6), :] for t in range(6)], axis=1)
    zero = jnp.zeros((6, WIDTH), F32)
    total = (a_ref[...] + b_ref[...]) + (c_ref[...] + d_ref[...])
    out_ref[0:6, :] = total[0:6] + jnp.where(core == 0, rest, zero)
    out_ref[6:12, :] = total[6:12] + jnp.where(core == 0, zero, rest)


def final_kernel(sc_ref, q_ref, k_ref, w_ref, x_ref, s_ref, dp_ref, ga_ref, layer_ref, dq0_ref, dk0_ref, dv0_ref,
                 out_ref, dq_ref, dk_ref, dv_ref, xs):
    row_start, tile_count = sc_ref[0], sc_ref[1]
    xs[...] = x_ref[...].astype(F32).reshape(PEERS * 16, LANES)
    lane = iota((16, LANES), 1)
    e_rows = [None] * 16
    dkv_rows = []
    for i in range(16):
        a, ii = i // 4, i % 4
        total = None
        for j in range(4):
            piece = xs[pl.ds(16 * j + i, 16, stride=64), :]
            total = piece if total is None else total + piece
            moved = piece if a == 3 else pltpu.roll(piece, 32 + 32 * a, 1)
            old = e_rows[4 * j + ii]
            e_rows[4 * j + ii] = moved if old is None else jnp.where((lane >> 5) == a, moved, old)
        dkv_rows.append(total)
    dkv = jnp.concatenate(dkv_rows, axis=0)
    e = jnp.concatenate(e_rows, axis=0)
    lane = iota((ROWS, LANES), 1)
    dkv = jnp.where(lane < 96, dkv, 0.0).astype(BF)
    lse = jnp.sum(jnp.where((lane >= 96) & (lane < 99), e, 0.0), axis=1, keepdims=True)
    e = jnp.where(lane < 96, e, 0.0).astype(BF)
    own = own_head_mask()
    own32 = own.astype(F32)
    first, second = unfold(0), unfold(HEAD_WIDTH)
    att = nn(e, second).astype(BF) * own
    valid_row = (row_start + iota((ROWS, WIDTH), 0)) < tile_count
    out_ref[...] = jnp.where(valid_row, layer_ref[...] + nn(att, w_ref[...]), 0.0).astype(BF)
    q_own = q_ref[...] * own
    ga_own = ga_ref[...]
    p = jnp.exp(s_ref[...] - lse)
    delta = jnp.sum(ga_own.astype(F32) * att.astype(F32), axis=1, keepdims=True)
    ds = (p * (dp_ref[...] - delta)).astype(BF)
    dq_ref[...] = (dq0_ref[...] + (nn(ds, k_ref[...]) * SCALE + nn(e, first)) * own32).astype(BF)
    dk_ref[...] = (dk0_ref[...] + tn(ds, q_own) * SCALE + nn(dkv, first) * own32).astype(BF)
    dv_ref[...] = (dv0_ref[...] + tn(p.astype(BF), ga_own) + nn(dkv, second) * own32).astype(BF)


def call(kernel, inputs, outs, scratch=(), scalars=False, near=(), keep=(), limit=LIMIT, **more):
    vmem = pl.BlockSpec(memory_space=pltpu.VMEM)
    smem = pl.BlockSpec(memory_space=pltpu.SMEM)
    put = pltpu.with_memory_space_constraint
    placed = [put(x, pltpu.VMEM if n + 1 in near else pltpu.HBM) for n, x in enumerate(inputs[1:])]
    shapes = [(pltpu.VMEM if n in keep else pltpu.HBM)(s, t) for n, (s, t) in enumerate(outs)]
    if scalars:
        shapes[-1] = jax.ShapeDtypeStruct(*outs[-1])
    settings = dict(
        in_specs=[smem] + [vmem] * len(placed),
        out_specs=[vmem] * (len(outs) - 1) + [smem if scalars else vmem],
    )
    settings.update(more)
    return pl.pallas_call(
        kernel,
        out_shape=shapes,
        scratch_shapes=[pltpu.VMEM(s, t) for s, t in scratch],
        compiler_params=pltpu.CompilerParams(vmem_limit_bytes=limit * 1024 * 1024),
        **settings,
    )(inputs[0], *placed)


def on_device(query_rows, key_rows, value_rows, grad_out, out_weight, tile_counts):
    q, k, v, g = query_rows[0], key_rows[0], value_rows[0], grad_out[0]
    place = lax.axis_index("seq")
    other_core = [(0, 1), (1, 0), (2, 3), (3, 2)]
    flat, tall = (ROWS, WIDTH), (WIDTH, ROWS)

    send, sc = call(
        pack_kernel, (tile_counts, q, k, v, g), [((PEERS, SEND_ROWS, LANES), BF), ((5,), jnp.int32)],
        [((PEERS * 16, LANES), F32), ((PEERS * 24, LANES), F32)], scalars=True,
    )
    x = lax.all_to_all(send, "seq", 0, 0)

    part = (PEERS, PART_ROWS, LANES)
    at0, lse0, keep, swap = call(
        forward_kernel, (sc, q, k, v, g), [(tall, BF), ((HEADS, ROWS), F32), (part, BF), (part, BF)],
        [(tall, BF), (tall, BF), ((6, WIDTH, LANES), F32), ((PEERS * PART_ROWS, LANES), F32)],
    )
    got = lax.ppermute(swap, "slide", other_core)
    (joined,) = call(join_kernel, (sc, keep, got), [((PEERS, BACK_ROWS, LANES), BF)])

    w_head = lax.dynamic_slice_in_dim(out_weight, place // 4 * HEAD_WIDTH, HEAD_WIDTH, 0)
    held = pl.BlockSpec(memory_space=pltpu.VMEM)
    whole = lambda *shape: pl.BlockSpec(shape, lambda i: (0,) * len(shape))
    back, strided = call(
        far_kernel,
        (sc, x, w_head, joined),
        [((PEERS, BACK_ROWS, LANES), BF), ((4, 12, WIDTH), F32)],
        [((PEERS * n, LANES), F32) for n in (16, 24, 16)],
        near=(1,),
        grid=(1,),
        in_specs=[
            pl.BlockSpec(memory_space=pltpu.SMEM),
            whole(PEERS, SEND_ROWS, LANES),
            whole(HEAD_WIDTH, WIDTH),
            pl.BlockSpec(memory_space=pl.ANY),
        ],
        out_specs=[whole(PEERS, 16, LANES), whole(4, 12, WIDTH)],
        input_output_aliases={3: 0},
    )
    y = lax.all_to_all(back, "seq", 0, 0)

    dq0, dk0, dv0, layer0, ga, s0, dp0, strided = call(
        backward_kernel, (sc, q, k, v, g, out_weight, at0, lse0, strided),
        [(flat, F32)] * 4 + [(flat, BF)] + [((ROWS, ROWS), F32)] * 2 + [((4, 12, WIDTH), F32)],
        [(tall, BF)] * 3 + [(tall, F32)] * 3,
        keep=(0, 1, 2),
    )
    quarter = place % 4
    pieces = []
    for step in range(4):
        mine = lax.dynamic_index_in_dim(strided, (quarter + step) % 4, 0, keepdims=False)
        ring = [(d, d // 4 * 4 + (d + step) % 4) for d in range(PEERS)]
        pieces.append(lax.ppermute(mine, "seq", ring) if step else mine)
    (weight,) = call(
        weight_kernel, (sc, y, *pieces), [((12, WIDTH), F32)], [((PART_ROWS, LANES), F32)], near=(1,)
    )
    others = [lax.ppermute(weight, "slide", [(n, n ^ bits) for n in range(4)]) for bits in (2, 3, 1)]

    outs = call(
        final_kernel,
        (sc, q, k, out_weight, y, s0, dp0, ga, layer0, dq0, dk0, dv0),
        [(flat, BF)] * 4,
        [((PEERS * 16, LANES), F32)],
        near=(4, 9, 10, 11),
        grid=(1,),
        in_specs=[pl.BlockSpec(memory_space=pltpu.SMEM)] + [held] * 3 + [whole(PEERS, 16, LANES)] + [held] * 7,
    )
    return tuple(o[None] for o in outs) + (weight + others[0] + others[1] + others[2],)


def solution(mesh):
    rows = P("slide", "seq", None)
    return jax.shard_map(
        on_device,
        mesh=mesh,
        in_specs=(rows, rows, rows, rows, P(), P("slide")),
        out_specs=(rows, rows, rows, rows, P("seq", None)),
        check_vma=False,
    )
```

```python
import jax
import jax.numpy as jnp
from jax import lax
from jax.experimental import pallas as pl
from jax.experimental.pallas import tpu as pltpu
from jax.sharding import PartitionSpec as P

HEADS = 16
HEAD_WIDTH = 48
ROWS = 256
WIDTH = 768
PEERS = 64
LANES = 128
SCALE = HEAD_WIDTH ** -0.5
MASKED = -1e30
BF = jnp.bfloat16
F32 = jnp.float32
SEND_ROWS = 40
BACK_ROWS = 56
PART_ROWS = 40
LIMIT = 48
GROUP = 4
POWER = SCALE * 1.4426950408889634


def iota(shape, dim):
    return lax.broadcasted_iota(jnp.int32, shape, dim)


def head_of(feature):
    return (feature * 1366) >> 16


def onehot(mask):
    return jnp.where(mask, 1.0, 0.0).astype(BF)


def nn(a, b):
    return lax.dot_general(a, b, (((1,), (0,)), ((), ())), preferred_element_type=F32)


def nt(a, b):
    return lax.dot_general(a, b, (((1,), (1,)), ((), ())), preferred_element_type=F32)


def tn(a, b):
    return lax.dot_general(a, b, (((0,), (0,)), ((), ())), preferred_element_type=F32)


def own_head_mask():
    return onehot(head_of(iota((ROWS, WIDTH), 1)) == (iota((ROWS, WIDTH), 0) & 15))


def fold(offset):
    f = iota((WIDTH, LANES), 0)
    lane = iota((WIDTH, LANES), 1) - offset
    return onehot((f - HEAD_WIDTH * head_of(f)) == lane)


def unfold(offset):
    f = iota((LANES, WIDTH), 1)
    lane = iota((LANES, WIDTH), 0) - offset
    return onehot((f - HEAD_WIDTH * head_of(f)) == lane)


def split3(x):
    hi = x.astype(BF).astype(F32)
    mid = (x - hi).astype(BF).astype(F32)
    return hi, mid, (x - hi - mid).astype(BF).astype(F32)


def pack_kernel(count_ref, q_ref, k_ref, v_ref, g_ref, out_ref, next_ref, rows, grads):
    row_start, tile_count = lax.axis_index("seq") * ROWS, count_ref[0]
    next_ref[...] = jnp.full(next_ref.shape, tile_count, jnp.int32)
    own = own_head_mask()
    q_own = q_ref[...] * own
    valid_key = (row_start + iota((ROWS, ROWS), 1)) < tile_count
    s = jnp.where(valid_key, nt(q_own, k_ref[...]) * SCALE, MASKED)
    m = jnp.max(s, axis=1, keepdims=True)
    p = jnp.exp(s - m)
    l = jnp.sum(p, axis=1, keepdims=True)
    o = (nn(p.astype(BF), v_ref[...]) * (1.0 / l)).astype(BF) * own
    hi, mid, lo = split3(m + jnp.log(l))
    first, second = fold(0), fold(HEAD_WIDTH)
    lane = iota((ROWS, LANES), 1)
    d = nn(q_own, first) + nn(o, second)
    d = jnp.where(lane == 96, hi, jnp.where(lane == 97, mid, jnp.where(lane == 98, lo, d)))
    c = nn(k_ref[...] * own, first) + nn(v_ref[...] * own, second)
    late = iota((16, LANES), 1) >= 96
    for a in range(4):
        turned = d if a == 3 else pltpu.roll(d, 96 - 32 * a, 1)
        for ii in range(4):
            i = 4 * a + ii
            for j in range(4):
                at = 16 * (4 * j + ii)
                rows[pl.ds(16 * j + i, 16, stride=64), :] = jnp.where(late, turned[at : at + 16], c[16 * i : 16 * i + 16])
    out_ref[:, 0:16, :] = rows[...].astype(BF).reshape(PEERS, 16, LANES)
    valid_row = (row_start + iota((ROWS, WIDTH), 0)) < tile_count
    g = jnp.where(valid_row, g_ref[...].astype(F32), 0.0)
    for j in range(4):
        for ii in range(4):
            at = 16 * (4 * j + ii)
            for t in range(6):
                grads[pl.ds(24 * j + 4 * t + ii, 16, stride=96), :] = g[at : at + 16, 128 * t : 128 * t + 128]
    out_ref[:, 16:40, :] = grads[...].astype(BF).reshape(PEERS, 24, LANES)


def head_window(h):
    f = HEAD_WIDTH * h
    a, b = f // LANES * LANES, -(-(f + HEAD_WIDTH) // LANES) * LANES
    lane = a + iota((ROWS, b - a), 1)
    return slice(a, b), slice(f, f + HEAD_WIDTH), onehot((lane >= f) & (lane < f + HEAD_WIDTH))


def forward_kernel(count_ref, q_ref, k_ref, v_ref, g_ref, at_ref, lse_ref, keep_ref, send_ref, qt, vt, big, part):
    row_start, tile_count, core = lax.axis_index("seq") * ROWS, count_ref[0:1, 0:1], lax.axis_index("slide") % 2
    valid_row = (row_start + iota((ROWS, WIDTH), 0)) < tile_count
    g = jnp.where(valid_row, g_ref[...].astype(F32), 0.0).astype(BF)
    qt[...] = q_ref[...].T
    vt[...] = v_ref[...].T
    valid_key = (row_start + iota((ROWS, ROWS), 0)) < tile_count
    column = iota((1, ROWS), 1) & 15
    for start in range(0, HEADS, GROUP):
        group = [(h, *head_window(h)) for h in range(start, start + GROUP)]
        scores = [jnp.where(valid_key, nn(k_ref[:, w] * here, qt[w, :]), MASKED) for _, w, _, here in group]
        tops = [jnp.max(s, axis=0, keepdims=True) * POWER for s in scores]
        probs = [jnp.exp2(s * POWER - m) for s, m in zip(scores, tops)]
        totals = [jnp.sum(p, axis=0, keepdims=True) for p in probs]
        sums = [nn(vt[rows, :], p.astype(BF)) for (_, _, rows, _), p in zip(group, probs)]
        for (h, _, rows, _), o, m, l in zip(group, sums, tops, totals):
            at_ref[rows, :] = (o * jnp.where(column == h, 0.0, 1.0 / l)).astype(BF)
            lse_ref[h : h + 1, :] = jnp.where(column == h, 1e30, m + jnp.log2(l))
    partial = nn(at_ref[...], g)
    for t in range(6):
        big[t] = partial[:, 128 * t : 128 * t + 128]
    zero = jnp.zeros((PEERS, LANES), F32)
    for i in range(36, PART_ROWS):
        part[pl.ds(i, PEERS, stride=PART_ROWS), :] = zero
    for ref, c in ((keep_ref, core), (send_ref, 1 - core)):
        for i in range(6):
            for t in range(6):
                part[pl.ds(6 * i + t, PEERS, stride=PART_ROWS), :] = big[t, pl.ds(6 * c + i, PEERS, stride=12), :]
        ref[...] = part[...].astype(BF).reshape(PEERS, PART_ROWS, LANES)


def join_kernel(keep_ref, got_ref, out_ref):
    out_ref[:, 0:16, :] = jnp.zeros((PEERS, 16, LANES), BF)
    out_ref[:, 16:56, :] = (keep_ref[...].astype(F32) + got_ref[...].astype(F32)).astype(BF)


def backward_kernel(count_ref, q_ref, k_ref, v_ref, g_ref, w_ref, at_ref, lse_ref, strided_ref,
                    dq_ref, dk_ref, dv_ref, layer_ref, ga_ref, s_ref, dp_ref, pass_ref, qt, kt, gat, dqt, dkt, dvt):
    row_start, tile_count = lax.axis_index("seq") * ROWS, count_ref[0:1, 0:1]
    pass_ref[...] = strided_ref[...]
    valid_row = (row_start + iota((ROWS, WIDTH), 0)) < tile_count
    g = jnp.where(valid_row, g_ref[...].astype(F32), 0.0).astype(BF)
    gat[...] = nt(w_ref[...], g).astype(BF)
    ga_row = nt(g, w_ref[...]).astype(BF)
    qt[...] = q_ref[...].T
    kt[...] = k_ref[...].T
    valid_key = (row_start + iota((ROWS, ROWS), 0)) < tile_count
    for start in range(0, HEADS, GROUP):
        group = [(h, *head_window(h)) for h in range(start, start + GROUP)]
        scores = [jnp.where(valid_key, nn(k_ref[:, w] * here, qt[w, :]), MASKED) for _, w, _, here in group]
        slopes = [nn(v_ref[:, w] * here, gat[w, :]) for _, w, _, here in group]
        probs = [jnp.exp2(s * POWER - lse_ref[h : h + 1, :]) for (h, _, _, _), s in zip(group, scores)]
        deltas = [
            jnp.sum(gat[rows, :].astype(F32) * at_ref[rows, :].astype(F32), axis=0, keepdims=True)
            for _, _, rows, _ in group
        ]
        steps = [(p * (dp - delta)).astype(BF) for p, dp, delta in zip(probs, slopes, deltas)]
        for (_, _, rows, _), p, ds in zip(group, probs, steps):
            dqt[rows, :] = nn(kt[rows, :], ds) * SCALE
            dkt[rows, :] = nt(qt[rows, :], ds) * SCALE
            dvt[rows, :] = nt(gat[rows, :], p.astype(BF))
    dq_ref[...] = dqt[...].T
    dk_ref[...] = dkt[...].T
    dv_ref[...] = dvt[...].T
    own = own_head_mask()
    ga_own = ga_row * own
    ga_ref[...] = ga_own
    layer_ref[...] = nn(at_ref[...].T, w_ref[...])
    valid_key = (row_start + iota((ROWS, ROWS), 1)) < tile_count
    s_ref[...] = jnp.where(valid_key, nt(q_ref[...] * own, k_ref[...]) * SCALE, MASKED)
    dp_ref[...] = nt(ga_own, v_ref[...])


def far_kernel(count_ref, x_ref, w_ref, joined_ref, back_ref, strided_ref, xs, gs, ps):
    tile_count, head = count_ref[0:1, 0:1], lax.axis_index("seq") // 4
    x = x_ref[:, 0:16, :].reshape(PEERS * 16, LANES)
    xs[...] = x.astype(F32)
    gs[...] = x_ref[:, 16:40, :].astype(F32).reshape(PEERS * 24, LANES)
    lane = iota((PEERS, LANES), 1)
    parts, grads = [], []
    for ii in range(4):
        total = jnp.zeros((PEERS, LANES), F32)
        for a in range(4):
            piece = xs[pl.ds(4 * a + ii, PEERS, stride=16), :]
            piece = piece if a == 3 else pltpu.roll(piece, 32 + 32 * a, 1)
            total = jnp.where((lane >> 5) == a, piece, total)
        parts.append(total)
        grads.append(jnp.concatenate([gs[pl.ds(4 * t + ii, PEERS, stride=24), :] for t in range(6)], axis=1))
    d = jnp.concatenate(parts, axis=0)
    g = jnp.concatenate(grads, axis=0).astype(BF)
    dt = d.T
    row = iota((LANES, ROWS), 0)
    q_t = jnp.where(row < 48, dt, 0.0).astype(BF)
    q_row = jnp.where(iota((ROWS, LANES), 1) < 48, d, 0.0).astype(BF)
    lse_near = jnp.sum(jnp.where((row >= 96) & (row < 99), dt, 0.0), axis=0, keepdims=True)
    valid_key = (16 * iota((PEERS * 16, ROWS), 0) + head) < tile_count
    s = jnp.where(valid_key, nn(x, q_t) * SCALE, MASKED)
    m = jnp.maximum(jnp.max(s, axis=0, keepdims=True), lse_near)
    p = jnp.exp(s - m)
    near = jnp.exp(lse_near - m)
    l = jnp.sum(p, axis=0, keepdims=True) + near
    inv = 1.0 / l
    xt = xs[...].T.astype(BF)
    middle = (row >= 48) & (row < 96)
    att = jnp.where(middle, (nn(xt, p.astype(BF)) + near * dt) * inv, 0.0).astype(BF)
    w_pad = jnp.concatenate([jnp.zeros((48, WIDTH), BF), w_ref[...], jnp.zeros((32, WIDTH), BF)], axis=0)
    ga_t = nt(w_pad, g)
    ga_row = ga_t.T.astype(BF)
    ga_t = ga_t.astype(BF)
    delta = jnp.sum(ga_t.astype(F32) * att.astype(F32), axis=0, keepdims=True)
    dp = nn(x, ga_t)
    p = p * inv
    ds = (p * (dp - delta)).astype(BF)
    dq = nn(xt, ds) * SCALE
    hi, mid, lo = split3(m + jnp.log(l))
    e = jnp.where(row < 48, dq, att.astype(F32))
    e = jnp.where(row == 96, hi, jnp.where(row == 97, mid, jnp.where(row == 98, lo, e)))
    e = e.T
    ps[...] = nn(ds, q_row) * SCALE + nn(p.astype(BF), ga_row)
    for a in range(4):
        turned = e if a == 3 else pltpu.roll(e, 96 - 32 * a, 1)
        for ii in range(4):
            at = pl.ds(4 * a + ii, PEERS, stride=16)
            ps[at, :] = jnp.where(lane >= 96, turned[64 * ii : 64 * ii + 64], ps[at, :])
    back_ref[...] = ps[...].astype(BF).reshape(PEERS, 16, LANES)
    partial = nn(att, g)
    for j in range(4):
        strided_ref[j] = partial[48 + 12 * j : 60 + 12 * j]


def weight_kernel(y_ref, a_ref, b_ref, c_ref, d_ref, out_ref, scr):
    core = lax.axis_index("slide") % 2
    scr[...] = jnp.sum(y_ref[:, 16:56, :].astype(F32), axis=0)
    rest = jnp.concatenate([scr[pl.ds(t, 6, stride=6), :] for t in range(6)], axis=1)
    zero = jnp.zeros((6, WIDTH), F32)
    total = (a_ref[...] + b_ref[...]) + (c_ref[...] + d_ref[...])
    out_ref[0:6, :] = total[0:6] + jnp.where(core == 0, rest, zero)
    out_ref[6:12, :] = total[6:12] + jnp.where(core == 0, zero, rest)


def final_kernel(count_ref, q_ref, k_ref, w_ref, x_ref, s_ref, dp_ref, ga_ref, layer_ref, dq0_ref, dk0_ref, dv0_ref,
                 out_ref, dq_ref, dk_ref, dv_ref, xs):
    row_start, tile_count = lax.axis_index("seq") * ROWS, count_ref[0:1, 0:1]
    xs[...] = x_ref[...].astype(F32).reshape(PEERS * 16, LANES)
    lane = iota((16, LANES), 1)
    e_rows = [None] * 16
    dkv_rows = []
    for i in range(16):
        a, ii = i // 4, i % 4
        total = None
        for j in range(4):
            piece = xs[pl.ds(16 * j + i, 16, stride=64), :]
            total = piece if total is None else total + piece
            moved = piece if a == 3 else pltpu.roll(piece, 32 + 32 * a, 1)
            old = e_rows[4 * j + ii]
            e_rows[4 * j + ii] = moved if old is None else jnp.where((lane >> 5) == a, moved, old)
        dkv_rows.append(total)
    dkv = jnp.concatenate(dkv_rows, axis=0)
    e = jnp.concatenate(e_rows, axis=0)
    lane = iota((ROWS, LANES), 1)
    dkv = jnp.where(lane < 96, dkv, 0.0).astype(BF)
    lse = jnp.sum(jnp.where((lane >= 96) & (lane < 99), e, 0.0), axis=1, keepdims=True)
    e = jnp.where(lane < 96, e, 0.0).astype(BF)
    own = own_head_mask()
    own32 = own.astype(F32)
    first, second = unfold(0), unfold(HEAD_WIDTH)
    att = nn(e, second).astype(BF) * own
    valid_row = (row_start + iota((ROWS, WIDTH), 0)) < tile_count
    out_ref[...] = jnp.where(valid_row, layer_ref[...] + nn(att, w_ref[...]), 0.0).astype(BF)
    q_own = q_ref[...] * own
    ga_own = ga_ref[...]
    p = jnp.exp(s_ref[...] - lse)
    delta = jnp.sum(ga_own.astype(F32) * att.astype(F32), axis=1, keepdims=True)
    ds = (p * (dp_ref[...] - delta)).astype(BF)
    dq_ref[...] = (dq0_ref[...] + (nn(ds, k_ref[...]) * SCALE + nn(e, first)) * own32).astype(BF)
    dk_ref[...] = (dk0_ref[...] + tn(ds, q_own) * SCALE + nn(dkv, first) * own32).astype(BF)
    dv_ref[...] = (dv0_ref[...] + tn(p.astype(BF), ga_own) + nn(dkv, second) * own32).astype(BF)


def call(kernel, inputs, outs, scratch=(), scalars=False, near=(), keep=(), limit=LIMIT, **more):
    vmem = pl.BlockSpec(memory_space=pltpu.VMEM)
    put = pltpu.with_memory_space_constraint
    placed = [put(x, pltpu.VMEM if n in near else pltpu.HBM) for n, x in enumerate(inputs)]
    specs = [vmem] * len(inputs)
    if scalars:
        placed[0], specs[0] = inputs[0], pl.BlockSpec(memory_space=pltpu.SMEM)
    settings = dict(in_specs=specs, out_specs=[vmem] * len(outs))
    settings.update(more)
    return pl.pallas_call(
        kernel,
        out_shape=[(pltpu.VMEM if n in keep else pltpu.HBM)(s, t) for n, (s, t) in enumerate(outs)],
        scratch_shapes=[pltpu.VMEM(s, t) for s, t in scratch],
        compiler_params=pltpu.CompilerParams(vmem_limit_bytes=limit * 1024 * 1024),
        **settings,
    )(*placed)


def on_device(query_rows, key_rows, value_rows, grad_out, out_weight, tile_counts):
    q, k, v, g = query_rows[0], key_rows[0], value_rows[0], grad_out[0]
    place = lax.axis_index("seq")
    other_core = [(0, 1), (1, 0), (2, 3), (3, 2)]
    flat, tall = (ROWS, WIDTH), (WIDTH, ROWS)

    send, count = call(
        pack_kernel, (tile_counts, q, k, v, g), [((PEERS, SEND_ROWS, LANES), BF), ((8, LANES), jnp.int32)],
        [((PEERS * 16, LANES), F32), ((PEERS * 24, LANES), F32)], keep=(0, 1), scalars=True,
    )
    x = lax.all_to_all(send, "seq", 0, 0)

    part = (PEERS, PART_ROWS, LANES)
    at0, lse0, keep, swap = call(
        forward_kernel, (count, q, k, v, g), [(tall, BF), ((HEADS, ROWS), F32), (part, BF), (part, BF)],
        [(tall, BF), (tall, BF), ((6, WIDTH, LANES), F32), ((PEERS * PART_ROWS, LANES), F32)],
        near=(0,),
    )
    got = lax.ppermute(swap, "slide", other_core)
    (joined,) = call(join_kernel, (keep, got), [((PEERS, BACK_ROWS, LANES), BF)], keep=(0,))

    w_head = lax.dynamic_slice_in_dim(out_weight, place // 4 * HEAD_WIDTH, HEAD_WIDTH, 0)
    held = pl.BlockSpec(memory_space=pltpu.VMEM)
    whole = lambda *shape: pl.BlockSpec(shape, lambda i: (0,) * len(shape))
    back, strided = call(
        far_kernel,
        (count, x, w_head, joined),
        [((PEERS, BACK_ROWS, LANES), BF), ((4, 12, WIDTH), F32)],
        [((PEERS * n, LANES), F32) for n in (16, 24, 16)],
        near=(0, 1, 2, 3),
        keep=(0,),
        grid=(1,),
        in_specs=[
            whole(8, LANES),
            whole(PEERS, SEND_ROWS, LANES),
            whole(HEAD_WIDTH, WIDTH),
            pl.BlockSpec(memory_space=pl.ANY),
        ],
        out_specs=[whole(PEERS, 16, LANES), whole(4, 12, WIDTH)],
        input_output_aliases={3: 0},
    )
    y = lax.all_to_all(back, "seq", 0, 0)

    dq0, dk0, dv0, layer0, ga, s0, dp0, strided = call(
        backward_kernel, (count, q, k, v, g, out_weight, at0, lse0, strided),
        [(flat, F32)] * 4 + [(flat, BF)] + [((ROWS, ROWS), F32)] * 2 + [((4, 12, WIDTH), F32)],
        [(tall, BF)] * 3 + [(tall, F32)] * 3,
        near=(0,),
        keep=(0, 1, 2),
    )
    quarter = place % 4
    pieces = []
    for step in range(4):
        mine = lax.dynamic_index_in_dim(strided, (quarter + step) % 4, 0, keepdims=False)
        ring = [(d, d // 4 * 4 + (d + step) % 4) for d in range(PEERS)]
        pieces.append(lax.ppermute(mine, "seq", ring) if step else mine)
    (weight,) = call(
        weight_kernel, (y, *pieces), [((12, WIDTH), F32)], [((PART_ROWS, LANES), F32)], near=(0, 1, 2, 3, 4), keep=(0,)
    )
    others = [lax.ppermute(weight, "slide", [(n, n ^ bits) for n in range(4)]) for bits in (2, 3, 1)]

    outs = call(
        final_kernel,
        (count, q, k, out_weight, y, s0, dp0, ga, layer0, dq0, dk0, dv0),
        [(flat, BF)] * 4,
        [((PEERS * 16, LANES), F32)],
        near=(0, 4, 9, 10, 11),
        grid=(1,),
        in_specs=[held] * 4 + [whole(PEERS, 16, LANES)] + [held] * 7,
    )
    return tuple(o[None] for o in outs) + (weight + others[0] + others[1] + others[2],)


def solution(mesh):
    rows = P("slide", "seq", None)
    return jax.shard_map(
        on_device,
        mesh=mesh,
        in_specs=(rows, rows, rows, rows, P(), P("slide")),
        out_specs=(rows, rows, rows, rows, P("seq", None)),
        check_vma=False,
    )
```

```python
import jax
import jax.numpy as jnp
from jax import lax
from jax.experimental import pallas as pl
from jax.experimental.pallas import tpu as pltpu
from jax.sharding import PartitionSpec as P

HEADS = 16
HEAD_WIDTH = 48
ROWS = 256
WIDTH = 768
PEERS = 64
LANES = 128
SCALE = HEAD_WIDTH ** -0.5
MASKED = -1e30
BF = jnp.bfloat16
F32 = jnp.float32
SEND_ROWS = 40
BACK_ROWS = 56
PART_ROWS = 40
LIMIT = 48
GROUP = 4
POWER = SCALE * 1.4426950408889634


def iota(shape, dim):
    return lax.broadcasted_iota(jnp.int32, shape, dim)


def head_of(feature):
    return (feature * 1366) >> 16


def onehot(mask):
    return jnp.where(mask, 1.0, 0.0).astype(BF)


def nn(a, b):
    return lax.dot_general(a, b, (((1,), (0,)), ((), ())), preferred_element_type=F32)


def nt(a, b):
    return lax.dot_general(a, b, (((1,), (1,)), ((), ())), preferred_element_type=F32)


def tn(a, b):
    return lax.dot_general(a, b, (((0,), (0,)), ((), ())), preferred_element_type=F32)


def own_head_mask():
    return onehot(head_of(iota((ROWS, WIDTH), 1)) == (iota((ROWS, WIDTH), 0) & 15))


def fold(offset):
    f = iota((WIDTH, LANES), 0)
    lane = iota((WIDTH, LANES), 1) - offset
    return onehot((f - HEAD_WIDTH * head_of(f)) == lane)


def unfold(offset):
    f = iota((LANES, WIDTH), 1)
    lane = iota((LANES, WIDTH), 0) - offset
    return onehot((f - HEAD_WIDTH * head_of(f)) == lane)


def split3(x):
    hi = x.astype(BF).astype(F32)
    mid = (x - hi).astype(BF).astype(F32)
    return hi, mid, (x - hi - mid).astype(BF).astype(F32)


def pack_kernel(count_ref, q_ref, k_ref, v_ref, g_ref, out_ref, next_ref, rows, grads):
    row_start, tile_count = lax.axis_index("seq") * ROWS, count_ref[0]
    next_ref[...] = jnp.full(next_ref.shape, tile_count, jnp.int32)
    own = own_head_mask()
    q_own = q_ref[...] * own
    valid_key = (row_start + iota((ROWS, ROWS), 1)) < tile_count
    s = jnp.where(valid_key, nt(q_own, k_ref[...]) * SCALE, MASKED)
    m = jnp.max(s, axis=1, keepdims=True)
    p = jnp.exp(s - m)
    l = jnp.sum(p, axis=1, keepdims=True)
    o = (nn(p.astype(BF), v_ref[...]) * (1.0 / l)).astype(BF) * own
    hi, mid, lo = split3(m + jnp.log(l))
    first, second = fold(0), fold(HEAD_WIDTH)
    lane = iota((ROWS, LANES), 1)
    d = nn(q_own, first) + nn(o, second)
    d = jnp.where(lane == 96, hi, jnp.where(lane == 97, mid, jnp.where(lane == 98, lo, d)))
    c = nn(k_ref[...] * own, first) + nn(v_ref[...] * own, second)
    late = iota((16, LANES), 1) >= 96
    for a in range(4):
        turned = d if a == 3 else pltpu.roll(d, 96 - 32 * a, 1)
        for ii in range(4):
            i = 4 * a + ii
            for j in range(4):
                at = 16 * (4 * j + ii)
                rows[pl.ds(16 * j + i, 16, stride=64), :] = jnp.where(late, turned[at : at + 16], c[16 * i : 16 * i + 16])
    out_ref[:, 0:16, :] = rows[0 : PEERS * 16, :].astype(BF).reshape(PEERS, 16, LANES)
    valid_row = (row_start + iota((ROWS, WIDTH), 0)) < tile_count
    g = jnp.where(valid_row, g_ref[...].astype(F32), 0.0)
    for j in range(4):
        for ii in range(4):
            at = 16 * (4 * j + ii)
            for t in range(6):
                grads[pl.ds(24 * j + 4 * t + ii, 16, stride=96), :] = g[at : at + 16, 128 * t : 128 * t + 128]
    out_ref[:, 16:40, :] = grads[0 : PEERS * 24, :].astype(BF).reshape(PEERS, 24, LANES)


def head_window(h):
    f = HEAD_WIDTH * h
    a, b = f // LANES * LANES, -(-(f + HEAD_WIDTH) // LANES) * LANES
    lane = a + iota((ROWS, b - a), 1)
    return slice(a, b), slice(f, f + HEAD_WIDTH), onehot((lane >= f) & (lane < f + HEAD_WIDTH))


def forward_kernel(count_ref, q_ref, k_ref, v_ref, g_ref, at_ref, lse_ref, keep_ref, send_ref, qt, vt, big, part):
    row_start, tile_count, core = lax.axis_index("seq") * ROWS, count_ref[0:1, 0:1], lax.axis_index("slide") % 2
    valid_row = (row_start + iota((ROWS, WIDTH), 0)) < tile_count
    g = jnp.where(valid_row, g_ref[...].astype(F32), 0.0).astype(BF)
    qt[...] = q_ref[...].T
    vt[...] = v_ref[...].T
    valid_key = (row_start + iota((ROWS, ROWS), 0)) < tile_count
    column = iota((1, ROWS), 1) & 15
    for start in range(0, HEADS, GROUP):
        group = [(h, *head_window(h)) for h in range(start, start + GROUP)]
        scores = [jnp.where(valid_key, nn(k_ref[:, w] * here, qt[w, :]), MASKED) for _, w, _, here in group]
        tops = [jnp.max(s, axis=0, keepdims=True) * POWER for s in scores]
        probs = [jnp.exp2(s * POWER - m) for s, m in zip(scores, tops)]
        totals = [jnp.sum(p, axis=0, keepdims=True) for p in probs]
        sums = [nn(vt[rows, :], p.astype(BF)) for (_, _, rows, _), p in zip(group, probs)]
        for (h, _, rows, _), o, m, l in zip(group, sums, tops, totals):
            at_ref[rows, :] = (o * jnp.where(column == h, 0.0, 1.0 / l)).astype(BF)
            lse_ref[h : h + 1, :] = jnp.where(column == h, 1e30, m + jnp.log2(l))
    partial = nn(at_ref[...], g)
    for t in range(6):
        big[t, 0:WIDTH, :] = partial[:, 128 * t : 128 * t + 128]
    zero = jnp.zeros((PEERS, LANES), F32)
    for i in range(36, PART_ROWS):
        part[pl.ds(i, PEERS, stride=PART_ROWS), :] = zero
    for ref, c in ((keep_ref, core), (send_ref, 1 - core)):
        for i in range(6):
            for t in range(6):
                part[pl.ds(6 * i + t, PEERS, stride=PART_ROWS), :] = big[t, pl.ds(6 * c + i, PEERS, stride=12), :]
        ref[...] = part[0 : PEERS * PART_ROWS, :].astype(BF).reshape(PEERS, PART_ROWS, LANES)


def join_kernel(keep_ref, got_ref, out_ref):
    out_ref[:, 0:16, :] = jnp.zeros((PEERS, 16, LANES), BF)
    out_ref[:, 16:56, :] = (keep_ref[...].astype(F32) + got_ref[...].astype(F32)).astype(BF)


def backward_kernel(count_ref, q_ref, k_ref, v_ref, g_ref, w_ref, at_ref, lse_ref, strided_ref,
                    dq_ref, dk_ref, dv_ref, layer_ref, ga_ref, s_ref, dp_ref, pass_ref, qt, kt, gat, dqt, dkt, dvt):
    row_start, tile_count = lax.axis_index("seq") * ROWS, count_ref[0:1, 0:1]
    pass_ref[...] = strided_ref[...]
    valid_row = (row_start + iota((ROWS, WIDTH), 0)) < tile_count
    g = jnp.where(valid_row, g_ref[...].astype(F32), 0.0).astype(BF)
    gat[...] = nt(w_ref[...], g).astype(BF)
    ga_row = nt(g, w_ref[...]).astype(BF)
    qt[...] = q_ref[...].T
    kt[...] = k_ref[...].T
    valid_key = (row_start + iota((ROWS, ROWS), 0)) < tile_count
    for start in range(0, HEADS, GROUP):
        group = [(h, *head_window(h)) for h in range(start, start + GROUP)]
        scores = [jnp.where(valid_key, nn(k_ref[:, w] * here, qt[w, :]), MASKED) for _, w, _, here in group]
        slopes = [nn(v_ref[:, w] * here, gat[w, :]) for _, w, _, here in group]
        probs = [jnp.exp2(s * POWER - lse_ref[h : h + 1, :]) for (h, _, _, _), s in zip(group, scores)]
        deltas = [
            jnp.sum(gat[rows, :].astype(F32) * at_ref[rows, :].astype(F32), axis=0, keepdims=True)
            for _, _, rows, _ in group
        ]
        steps = [(p * (dp - delta)).astype(BF) for p, dp, delta in zip(probs, slopes, deltas)]
        for (_, _, rows, _), p, ds in zip(group, probs, steps):
            dqt[rows, :] = nn(kt[rows, :], ds) * SCALE
            dkt[rows, :] = nt(qt[rows, :], ds) * SCALE
            dvt[rows, :] = nt(gat[rows, :], p.astype(BF))
    dq_ref[...] = dqt[...].T
    dk_ref[...] = dkt[...].T
    dv_ref[...] = dvt[...].T
    own = own_head_mask()
    ga_own = ga_row * own
    ga_ref[...] = ga_own
    layer_ref[...] = nn(at_ref[...].T, w_ref[...])
    valid_key = (row_start + iota((ROWS, ROWS), 1)) < tile_count
    s_ref[...] = jnp.where(valid_key, nt(q_ref[...] * own, k_ref[...]) * SCALE, MASKED)
    dp_ref[...] = nt(ga_own, v_ref[...])


def far_kernel(count_ref, x_ref, w_ref, joined_ref, back_ref, strided_ref, xs, gs, ps):
    tile_count, head = count_ref[0:1, 0:1], lax.axis_index("seq") // 4
    x = x_ref[:, 0:16, :].reshape(PEERS * 16, LANES)
    xs[0 : PEERS * 16, :] = x.astype(F32)
    gs[0 : PEERS * 24, :] = x_ref[:, 16:40, :].astype(F32).reshape(PEERS * 24, LANES)
    lane = iota((PEERS, LANES), 1)
    parts, grads = [], []
    for ii in range(4):
        total = jnp.zeros((PEERS, LANES), F32)
        for a in range(4):
            piece = xs[pl.ds(4 * a + ii, PEERS, stride=16), :]
            piece = piece if a == 3 else pltpu.roll(piece, 32 + 32 * a, 1)
            total = jnp.where((lane >> 5) == a, piece, total)
        parts.append(total)
        grads.append(jnp.concatenate([gs[pl.ds(4 * t + ii, PEERS, stride=24), :] for t in range(6)], axis=1))
    d = jnp.concatenate(parts, axis=0)
    g = jnp.concatenate(grads, axis=0).astype(BF)
    dt = d.T
    row = iota((LANES, ROWS), 0)
    q_t = jnp.where(row < 48, dt, 0.0).astype(BF)
    q_row = jnp.where(iota((ROWS, LANES), 1) < 48, d, 0.0).astype(BF)
    lse_near = jnp.sum(jnp.where((row >= 96) & (row < 99), dt, 0.0), axis=0, keepdims=True)
    valid_key = (16 * iota((PEERS * 16, ROWS), 0) + head) < tile_count
    s = jnp.where(valid_key, nn(x, q_t) * SCALE, MASKED)
    m = jnp.maximum(jnp.max(s, axis=0, keepdims=True), lse_near)
    p = jnp.exp(s - m)
    near = jnp.exp(lse_near - m)
    l = jnp.sum(p, axis=0, keepdims=True) + near
    inv = 1.0 / l
    xt = xs[0 : PEERS * 16, :].T.astype(BF)
    middle = (row >= 48) & (row < 96)
    att = jnp.where(middle, (nn(xt, p.astype(BF)) + near * dt) * inv, 0.0).astype(BF)
    w_pad = jnp.concatenate([jnp.zeros((48, WIDTH), BF), w_ref[...], jnp.zeros((32, WIDTH), BF)], axis=0)
    ga_t = nt(w_pad, g)
    ga_row = ga_t.T.astype(BF)
    ga_t = ga_t.astype(BF)
    delta = jnp.sum(ga_t.astype(F32) * att.astype(F32), axis=0, keepdims=True)
    dp = nn(x, ga_t)
    p = p * inv
    ds = (p * (dp - delta)).astype(BF)
    dq = nn(xt, ds) * SCALE
    hi, mid, lo = split3(m + jnp.log(l))
    e = jnp.where(row < 48, dq, att.astype(F32))
    e = jnp.where(row == 96, hi, jnp.where(row == 97, mid, jnp.where(row == 98, lo, e)))
    e = e.T
    ps[0 : PEERS * 16, :] = nn(ds, q_row) * SCALE + nn(p.astype(BF), ga_row)
    for a in range(4):
        turned = e if a == 3 else pltpu.roll(e, 96 - 32 * a, 1)
        for ii in range(4):
            at = pl.ds(4 * a + ii, PEERS, stride=16)
            ps[at, :] = jnp.where(lane >= 96, turned[64 * ii : 64 * ii + 64], ps[at, :])
    back_ref[...] = ps[0 : PEERS * 16, :].astype(BF).reshape(PEERS, 16, LANES)
    partial = nn(att, g)
    for j in range(4):
        strided_ref[j] = partial[48 + 12 * j : 60 + 12 * j]


def weight_kernel(y_ref, a_ref, b_ref, c_ref, d_ref, out_ref, scr):
    core = lax.axis_index("slide") % 2
    scr[0:PART_ROWS, :] = jnp.sum(y_ref[:, 16:56, :].astype(F32), axis=0)
    rest = jnp.concatenate([scr[pl.ds(t, 6, stride=6), :] for t in range(6)], axis=1)
    zero = jnp.zeros((6, WIDTH), F32)
    total = (a_ref[...] + b_ref[...]) + (c_ref[...] + d_ref[...])
    out_ref[0:6, :] = total[0:6] + jnp.where(core == 0, rest, zero)
    out_ref[6:12, :] = total[6:12] + jnp.where(core == 0, zero, rest)


def final_kernel(count_ref, q_ref, k_ref, w_ref, x_ref, s_ref, dp_ref, ga_ref, layer_ref, dq0_ref, dk0_ref, dv0_ref,
                 out_ref, dq_ref, dk_ref, dv_ref, xs):
    row_start, tile_count = lax.axis_index("seq") * ROWS, count_ref[0:1, 0:1]
    xs[0 : PEERS * 16, :] = x_ref[...].astype(F32).reshape(PEERS * 16, LANES)
    lane = iota((16, LANES), 1)
    e_rows = [None] * 16
    dkv_rows = []
    for i in range(16):
        a, ii = i // 4, i % 4
        total = None
        for j in range(4):
            piece = xs[pl.ds(16 * j + i, 16, stride=64), :]
            total = piece if total is None else total + piece
            moved = piece if a == 3 else pltpu.roll(piece, 32 + 32 * a, 1)
            old = e_rows[4 * j + ii]
            e_rows[4 * j + ii] = moved if old is None else jnp.where((lane >> 5) == a, moved, old)
        dkv_rows.append(total)
    dkv = jnp.concatenate(dkv_rows, axis=0)
    e = jnp.concatenate(e_rows, axis=0)
    lane = iota((ROWS, LANES), 1)
    dkv = jnp.where(lane < 96, dkv, 0.0).astype(BF)
    lse = jnp.sum(jnp.where((lane >= 96) & (lane < 99), e, 0.0), axis=1, keepdims=True)
    e = jnp.where(lane < 96, e, 0.0).astype(BF)
    own = own_head_mask()
    own32 = own.astype(F32)
    first, second = unfold(0), unfold(HEAD_WIDTH)
    att = nn(e, second).astype(BF) * own
    valid_row = (row_start + iota((ROWS, WIDTH), 0)) < tile_count
    out_ref[...] = jnp.where(valid_row, layer_ref[...] + nn(att, w_ref[...]), 0.0).astype(BF)
    q_own = q_ref[...] * own
    ga_own = ga_ref[...]
    p = jnp.exp(s_ref[...] - lse)
    delta = jnp.sum(ga_own.astype(F32) * att.astype(F32), axis=1, keepdims=True)
    ds = (p * (dp_ref[...] - delta)).astype(BF)
    dq_ref[...] = (dq0_ref[...] + (nn(ds, k_ref[...]) * SCALE + nn(e, first)) * own32).astype(BF)
    dk_ref[...] = (dk0_ref[...] + tn(ds, q_own) * SCALE + nn(dkv, first) * own32).astype(BF)
    dv_ref[...] = (dv0_ref[...] + tn(p.astype(BF), ga_own) + nn(dkv, second) * own32).astype(BF)


def call(kernel, inputs, outs, scratch=(), scalars=False, near=(), keep=(), limit=LIMIT, **more):
    vmem = pl.BlockSpec(memory_space=pltpu.VMEM)
    put = pltpu.with_memory_space_constraint
    placed = [put(x, pltpu.VMEM if n in near else pltpu.HBM) for n, x in enumerate(inputs)]
    specs = [vmem] * len(inputs)
    if scalars:
        placed[0], specs[0] = inputs[0], pl.BlockSpec(memory_space=pltpu.SMEM)
    settings = dict(in_specs=specs, out_specs=[vmem] * len(outs))
    settings.update(more)
    return pl.pallas_call(
        kernel,
        out_shape=[(pltpu.VMEM if n in keep else pltpu.HBM)(s, t) for n, (s, t) in enumerate(outs)],
        scratch_shapes=[pltpu.VMEM(s, t) for s, t in scratch],
        compiler_params=pltpu.CompilerParams(vmem_limit_bytes=limit * 1024 * 1024),
        **settings,
    )(*placed)


def on_device(query_rows, key_rows, value_rows, grad_out, out_weight, tile_counts):
    q, k, v, g = query_rows[0], key_rows[0], value_rows[0], grad_out[0]
    place = lax.axis_index("seq")
    other_core = [(0, 1), (1, 0), (2, 3), (3, 2)]
    flat, tall = (ROWS, WIDTH), (WIDTH, ROWS)

    send, count = call(
        pack_kernel, (tile_counts, q, k, v, g), [((PEERS, SEND_ROWS, LANES), BF), ((8, LANES), jnp.int32)],
        [((PEERS * 16 + 64, LANES), F32), ((PEERS * 24 + 96, LANES), F32)], keep=(0, 1), scalars=True,
    )
    x = lax.all_to_all(send, "seq", 0, 0)

    part = (PEERS, PART_ROWS, LANES)
    at0, lse0, keep, swap = call(
        forward_kernel, (count, q, k, v, g), [(tall, BF), ((HEADS, ROWS), F32), (part, BF), (part, BF)],
        [(tall, BF), (tall, BF), ((6, WIDTH + 16, LANES), F32), (((PEERS + 1) * PART_ROWS, LANES), F32)],
        near=(0,),
    )
    got = lax.ppermute(swap, "slide", other_core)
    (joined,) = call(join_kernel, (keep, got), [((PEERS, BACK_ROWS, LANES), BF)], keep=(0,))

    w_head = lax.dynamic_slice_in_dim(out_weight, place // 4 * HEAD_WIDTH, HEAD_WIDTH, 0)
    held = pl.BlockSpec(memory_space=pltpu.VMEM)
    whole = lambda *shape: pl.BlockSpec(shape, lambda i: (0,) * len(shape))
    back, strided = call(
        far_kernel,
        (count, x, w_head, joined),
        [((PEERS, BACK_ROWS, LANES), BF), ((4, 12, WIDTH), F32)],
        [(((PEERS + 1) * n, LANES), F32) for n in (16, 24, 16)],
        near=(0, 1, 2, 3),
        keep=(0,),
        grid=(1,),
        in_specs=[
            whole(8, LANES),
            whole(PEERS, SEND_ROWS, LANES),
            whole(HEAD_WIDTH, WIDTH),
            pl.BlockSpec(memory_space=pl.ANY),
        ],
        out_specs=[whole(PEERS, 16, LANES), whole(4, 12, WIDTH)],
        input_output_aliases={3: 0},
    )
    y = lax.all_to_all(back, "seq", 0, 0)

    dq0, dk0, dv0, layer0, ga, s0, dp0, strided = call(
        backward_kernel, (count, q, k, v, g, out_weight, at0, lse0, strided),
        [(flat, F32)] * 4 + [(flat, BF)] + [((ROWS, ROWS), F32)] * 2 + [((4, 12, WIDTH), F32)],
        [(tall, BF)] * 3 + [(tall, F32)] * 3,
        near=(0,),
        keep=(0, 1, 2),
    )
    quarter = place % 4
    pieces = []
    for step in range(4):
        mine = lax.dynamic_index_in_dim(strided, (quarter + step) % 4, 0, keepdims=False)
        ring = [(d, d // 4 * 4 + (d + step) % 4) for d in range(PEERS)]
        pieces.append(lax.ppermute(mine, "seq", ring) if step else mine)
    (weight,) = call(
        weight_kernel, (y, *pieces), [((12, WIDTH), F32)], [((PART_ROWS + 8, LANES), F32)], near=(0, 1, 2, 3, 4), keep=(0,)
    )
    others = [lax.ppermute(weight, "slide", [(n, n ^ bits) for n in range(4)]) for bits in (2, 3, 1)]

    outs = call(
        final_kernel,
        (count, q, k, out_weight, y, s0, dp0, ga, layer0, dq0, dk0, dv0),
        [(flat, BF)] * 4,
        [((PEERS * 16 + 64, LANES), F32)],
        near=(0, 4, 9, 10, 11),
        grid=(1,),
        in_specs=[held] * 4 + [whole(PEERS, 16, LANES)] + [held] * 7,
    )
    return tuple(o[None] for o in outs) + (weight + others[0] + others[1] + others[2],)


def solution(mesh):
    rows = P("slide", "seq", None)
    return jax.shard_map(
        on_device,
        mesh=mesh,
        in_specs=(rows, rows, rows, rows, P(), P("slide")),
        out_specs=(rows, rows, rows, rows, P("seq", None)),
        check_vma=False,
    )
```

```python
import jax
import jax.numpy as jnp
from jax import lax
from jax.experimental import pallas as pl
from jax.experimental.pallas import tpu as pltpu
from jax.sharding import PartitionSpec as P

HEADS = 16
HEAD_WIDTH = 48
ROWS = 256
WIDTH = 768
PEERS = 64
LANES = 128
SCALE = HEAD_WIDTH ** -0.5
MASKED = -1e30
BF = jnp.bfloat16
F32 = jnp.float32
SEND_ROWS = 40
BACK_ROWS = 56
PART_ROWS = 40
LIMIT = 48
GROUP = 4


def iota(shape, dim):
    return lax.broadcasted_iota(jnp.int32, shape, dim)


def head_of(feature):
    return (feature * 1366) >> 16


def onehot(mask):
    return jnp.where(mask, 1.0, 0.0).astype(BF)


def nn(a, b):
    return lax.dot_general(a, b, (((1,), (0,)), ((), ())), preferred_element_type=F32)


def nt(a, b):
    return lax.dot_general(a, b, (((1,), (1,)), ((), ())), preferred_element_type=F32)


def tn(a, b):
    return lax.dot_general(a, b, (((0,), (0,)), ((), ())), preferred_element_type=F32)


def own_head_mask():
    return onehot(head_of(iota((ROWS, WIDTH), 1)) == (iota((ROWS, WIDTH), 0) & 15))


def fold(offset):
    f = iota((WIDTH, LANES), 0)
    lane = iota((WIDTH, LANES), 1) - offset
    return onehot((f - HEAD_WIDTH * head_of(f)) == lane)


def unfold(offset):
    f = iota((LANES, WIDTH), 1)
    lane = iota((LANES, WIDTH), 0) - offset
    return onehot((f - HEAD_WIDTH * head_of(f)) == lane)


def split3(x):
    hi = x.astype(BF).astype(F32)
    mid = (x - hi).astype(BF).astype(F32)
    return hi, mid, (x - hi - mid).astype(BF).astype(F32)


def pack_kernel(count_ref, q_ref, k_ref, v_ref, g_ref, out_ref, next_ref, rows, grads):
    row_start, tile_count = lax.axis_index("seq") * ROWS, count_ref[0]
    next_ref[...] = jnp.full(next_ref.shape, tile_count, jnp.int32)
    own = own_head_mask()
    q_own = q_ref[...] * own
    valid_key = (row_start + iota((ROWS, ROWS), 1)) < tile_count
    s = jnp.where(valid_key, nt(q_own, k_ref[...]) * SCALE, MASKED)
    m = jnp.max(s, axis=1, keepdims=True)
    p = jnp.exp(s - m)
    l = jnp.sum(p, axis=1, keepdims=True)
    o = (nn(p.astype(BF), v_ref[...]) * (1.0 / l)).astype(BF) * own
    hi, mid, lo = split3(m + jnp.log(l))
    first, second = fold(0), fold(HEAD_WIDTH)
    lane = iota((ROWS, LANES), 1)
    d = nn(q_own, first) + nn(o, second)
    d = jnp.where(lane == 96, hi, jnp.where(lane == 97, mid, jnp.where(lane == 98, lo, d)))
    c = nn(k_ref[...] * own, first) + nn(v_ref[...] * own, second)
    late = iota((16, LANES), 1) >= 96
    for a in range(4):
        turned = d if a == 3 else pltpu.roll(d, 96 - 32 * a, 1)
        for ii in range(4):
            i = 4 * a + ii
            for j in range(4):
                at = 16 * (4 * j + ii)
                rows[pl.ds(16 * j + i, 16, stride=64), :] = jnp.where(late, turned[at : at + 16], c[16 * i : 16 * i + 16])
    out_ref[:, 0:16, :] = rows[0 : PEERS * 16, :].astype(BF).reshape(PEERS, 16, LANES)
    valid_row = (row_start + iota((ROWS, WIDTH), 0)) < tile_count
    g = jnp.where(valid_row, g_ref[...].astype(F32), 0.0)
    for j in range(4):
        for ii in range(4):
            at = 16 * (4 * j + ii)
            for t in range(6):
                grads[pl.ds(24 * j + 4 * t + ii, 16, stride=96), :] = g[at : at + 16, 128 * t : 128 * t + 128]
    out_ref[:, 16:40, :] = grads[0 : PEERS * 24, :].astype(BF).reshape(PEERS, 24, LANES)


def head_window(h):
    f = HEAD_WIDTH * h
    a, b = f // LANES * LANES, -(-(f + HEAD_WIDTH) // LANES) * LANES
    lane = a + iota((ROWS, b - a), 1)
    return slice(a, b), slice(f, f + HEAD_WIDTH), onehot((lane >= f) & (lane < f + HEAD_WIDTH))


def forward_kernel(count_ref, q_ref, k_ref, v_ref, g_ref, at_ref, stat_ref, keep_ref, send_ref, qt, vt, big, part):
    row_start, tile_count, core = lax.axis_index("seq") * ROWS, count_ref[0:1, 0:1], lax.axis_index("slide") % 2
    valid_row = (row_start + iota((ROWS, WIDTH), 0)) < tile_count
    g = jnp.where(valid_row, g_ref[...].astype(F32), 0.0).astype(BF)
    qt[...] = q_ref[...].T
    vt[...] = v_ref[...].T
    valid_key = (row_start + iota((ROWS, ROWS), 0)) < tile_count
    column = iota((1, ROWS), 1) & 15
    for start in range(0, HEADS, GROUP):
        group = [(h, *head_window(h)) for h in range(start, start + GROUP)]
        scores = [jnp.where(valid_key, nn(k_ref[:, w] * here, qt[w, :]) * SCALE, MASKED) for _, w, _, here in group]
        tops = [jnp.max(s, axis=0, keepdims=True) for s in scores]
        probs = [jnp.exp(s - m) for s, m in zip(scores, tops)]
        totals = [jnp.sum(p, axis=0, keepdims=True) for p in probs]
        sums = [nn(vt[rows, :], p.astype(BF)) for (_, _, rows, _), p in zip(group, probs)]
        for (h, _, rows, _), o, m, l in zip(group, sums, tops, totals):
            inv = jnp.where(column == h, 0.0, 1.0 / l)
            at_ref[rows, :] = (o * inv).astype(BF)
            stat_ref[h : h + 1, :] = m
            stat_ref[HEADS + h : HEADS + h + 1, :] = inv
    partial = nn(at_ref[...], g)
    for t in range(6):
        big[t, 0:WIDTH, :] = partial[:, 128 * t : 128 * t + 128]
    zero = jnp.zeros((PEERS, LANES), F32)
    for i in range(36, PART_ROWS):
        part[pl.ds(i, PEERS, stride=PART_ROWS), :] = zero
    for ref, c in ((keep_ref, core), (send_ref, 1 - core)):
        for i in range(6):
            for t in range(6):
                part[pl.ds(6 * i + t, PEERS, stride=PART_ROWS), :] = big[t, pl.ds(6 * c + i, PEERS, stride=12), :]
        ref[...] = part[0 : PEERS * PART_ROWS, :].astype(BF).reshape(PEERS, PART_ROWS, LANES)


def join_kernel(keep_ref, got_ref, out_ref):
    out_ref[:, 0:16, :] = jnp.zeros((PEERS, 16, LANES), BF)
    out_ref[:, 16:56, :] = (keep_ref[...].astype(F32) + got_ref[...].astype(F32)).astype(BF)


def backward_kernel(count_ref, q_ref, k_ref, v_ref, g_ref, w_ref, at_ref, stat_ref, strided_ref,
                    dq_ref, dk_ref, dv_ref, layer_ref, ga_ref, s_ref, dp_ref, pass_ref, qt, kt, gat, dqt, dkt, dvt):
    row_start, tile_count = lax.axis_index("seq") * ROWS, count_ref[0:1, 0:1]
    pass_ref[...] = strided_ref[...]
    valid_row = (row_start + iota((ROWS, WIDTH), 0)) < tile_count
    g = jnp.where(valid_row, g_ref[...].astype(F32), 0.0).astype(BF)
    gat[...] = nt(w_ref[...], g).astype(BF)
    ga_row = nt(g, w_ref[...]).astype(BF)
    qt[...] = q_ref[...].T
    kt[...] = k_ref[...].T
    valid_key = (row_start + iota((ROWS, ROWS), 0)) < tile_count
    for start in range(0, HEADS, GROUP):
        group = [(h, *head_window(h)) for h in range(start, start + GROUP)]
        scores = [jnp.where(valid_key, nn(k_ref[:, w] * here, qt[w, :]) * SCALE, MASKED) for _, w, _, here in group]
        slopes = [nn(v_ref[:, w] * here, gat[w, :]) for _, w, _, here in group]
        probs = [jnp.exp(s - stat_ref[h : h + 1, :]) * stat_ref[HEADS + h : HEADS + h + 1, :] for (h, _, _, _), s in zip(group, scores)]
        deltas = [
            jnp.sum(gat[rows, :].astype(F32) * at_ref[rows, :].astype(F32), axis=0, keepdims=True)
            for _, _, rows, _ in group
        ]
        steps = [(p * (dp - delta)).astype(BF) for p, dp, delta in zip(probs, slopes, deltas)]
        for (_, _, rows, _), p, ds in zip(group, probs, steps):
            dqt[rows, :] = nn(kt[rows, :], ds) * SCALE
            dkt[rows, :] = nt(qt[rows, :], ds) * SCALE
            dvt[rows, :] = nt(gat[rows, :], p.astype(BF))
    dq_ref[...] = dqt[...].T
    dk_ref[...] = dkt[...].T
    dv_ref[...] = dvt[...].T
    own = own_head_mask()
    ga_own = ga_row * own
    ga_ref[...] = ga_own
    layer_ref[...] = nn(at_ref[...].T, w_ref[...])
    valid_key = (row_start + iota((ROWS, ROWS), 1)) < tile_count
    s_ref[...] = jnp.where(valid_key, nt(q_ref[...] * own, k_ref[...]) * SCALE, MASKED)
    dp_ref[...] = nt(ga_own, v_ref[...])


def far_kernel(count_ref, x_ref, w_ref, joined_ref, back_ref, strided_ref, xs, gs, ps):
    tile_count, head = count_ref[0:1, 0:1], lax.axis_index("seq") // 4
    x = x_ref[:, 0:16, :].reshape(PEERS * 16, LANES)
    xs[0 : PEERS * 16, :] = x.astype(F32)
    gs[0 : PEERS * 24, :] = x_ref[:, 16:40, :].astype(F32).reshape(PEERS * 24, LANES)
    lane = iota((PEERS, LANES), 1)
    parts, grads = [], []
    for ii in range(4):
        total = jnp.zeros((PEERS, LANES), F32)
        for a in range(4):
            piece = xs[pl.ds(4 * a + ii, PEERS, stride=16), :]
            piece = piece if a == 3 else pltpu.roll(piece, 32 + 32 * a, 1)
            total = jnp.where((lane >> 5) == a, piece, total)
        parts.append(total)
        grads.append(jnp.concatenate([gs[pl.ds(4 * t + ii, PEERS, stride=24), :] for t in range(6)], axis=1))
    d = jnp.concatenate(parts, axis=0)
    g = jnp.concatenate(grads, axis=0).astype(BF)
    dt = d.T
    row = iota((LANES, ROWS), 0)
    q_t = jnp.where(row < 48, dt, 0.0).astype(BF)
    q_row = jnp.where(iota((ROWS, LANES), 1) < 48, d, 0.0).astype(BF)
    lse_near = jnp.sum(jnp.where((row >= 96) & (row < 99), dt, 0.0), axis=0, keepdims=True)
    valid_key = (16 * iota((PEERS * 16, ROWS), 0) + head) < tile_count
    s = jnp.where(valid_key, nn(x, q_t) * SCALE, MASKED)
    m = jnp.maximum(jnp.max(s, axis=0, keepdims=True), lse_near)
    p = jnp.exp(s - m)
    near = jnp.exp(lse_near - m)
    l = jnp.sum(p, axis=0, keepdims=True) + near
    inv = 1.0 / l
    xt = xs[0 : PEERS * 16, :].T.astype(BF)
    middle = (row >= 48) & (row < 96)
    att = jnp.where(middle, (nn(xt, p.astype(BF)) + near * dt) * inv, 0.0).astype(BF)
    w_pad = jnp.concatenate([jnp.zeros((48, WIDTH), BF), w_ref[...], jnp.zeros((32, WIDTH), BF)], axis=0)
    ga_t = nt(w_pad, g)
    ga_row = ga_t.T.astype(BF)
    ga_t = ga_t.astype(BF)
    delta = jnp.sum(ga_t.astype(F32) * att.astype(F32), axis=0, keepdims=True)
    dp = nn(x, ga_t)
    p = p * inv
    ds = (p * (dp - delta)).astype(BF)
    dq = nn(xt, ds) * SCALE
    hi, mid, lo = split3(m + jnp.log(l))
    e = jnp.where(row < 48, dq, att.astype(F32))
    e = jnp.where(row == 96, hi, jnp.where(row == 97, mid, jnp.where(row == 98, lo, e)))
    e = e.T
    ps[0 : PEERS * 16, :] = nn(ds, q_row) * SCALE + nn(p.astype(BF), ga_row)
    for a in range(4):
        turned = e if a == 3 else pltpu.roll(e, 96 - 32 * a, 1)
        for ii in range(4):
            at = pl.ds(4 * a + ii, PEERS, stride=16)
            ps[at, :] = jnp.where(lane >= 96, turned[64 * ii : 64 * ii + 64], ps[at, :])
    back_ref[...] = ps[0 : PEERS * 16, :].astype(BF).reshape(PEERS, 16, LANES)
    partial = nn(att, g)
    for j in range(4):
        strided_ref[j] = partial[48 + 12 * j : 60 + 12 * j]


def weight_kernel(y_ref, a_ref, b_ref, c_ref, d_ref, out_ref, scr):
    core = lax.axis_index("slide") % 2
    scr[0:PART_ROWS, :] = jnp.sum(y_ref[:, 16:56, :].astype(F32), axis=0)
    rest = jnp.concatenate([scr[pl.ds(t, 6, stride=6), :] for t in range(6)], axis=1)
    zero = jnp.zeros((6, WIDTH), F32)
    total = (a_ref[...] + b_ref[...]) + (c_ref[...] + d_ref[...])
    out_ref[0:6, :] = total[0:6] + jnp.where(core == 0, rest, zero)
    out_ref[6:12, :] = total[6:12] + jnp.where(core == 0, zero, rest)


def final_kernel(count_ref, q_ref, k_ref, w_ref, x_ref, s_ref, dp_ref, ga_ref, layer_ref, dq0_ref, dk0_ref, dv0_ref,
                 out_ref, dq_ref, dk_ref, dv_ref, xs):
    row_start, tile_count = lax.axis_index("seq") * ROWS, count_ref[0:1, 0:1]
    xs[0 : PEERS * 16, :] = x_ref[...].astype(F32).reshape(PEERS * 16, LANES)
    lane = iota((16, LANES), 1)
    e_rows = [None] * 16
    dkv_rows = []
    for i in range(16):
        a, ii = i // 4, i % 4
        total = None
        for j in range(4):
            piece = xs[pl.ds(16 * j + i, 16, stride=64), :]
            total = piece if total is None else total + piece
            moved = piece if a == 3 else pltpu.roll(piece, 32 + 32 * a, 1)
            old = e_rows[4 * j + ii]
            e_rows[4 * j + ii] = moved if old is None else jnp.where((lane >> 5) == a, moved, old)
        dkv_rows.append(total)
    dkv = jnp.concatenate(dkv_rows, axis=0)
    e = jnp.concatenate(e_rows, axis=0)
    lane = iota((ROWS, LANES), 1)
    dkv = jnp.where(lane < 96, dkv, 0.0).astype(BF)
    lse = jnp.sum(jnp.where((lane >= 96) & (lane < 99), e, 0.0), axis=1, keepdims=True)
    e = jnp.where(lane < 96, e, 0.0).astype(BF)
    own = own_head_mask()
    own32 = own.astype(F32)
    first, second = unfold(0), unfold(HEAD_WIDTH)
    att = nn(e, second).astype(BF) * own
    valid_row = (row_start + iota((ROWS, WIDTH), 0)) < tile_count
    out_ref[...] = jnp.where(valid_row, layer_ref[...] + nn(att, w_ref[...]), 0.0).astype(BF)
    q_own = q_ref[...] * own
    ga_own = ga_ref[...]
    p = jnp.exp(s_ref[...] - lse)
    delta = jnp.sum(ga_own.astype(F32) * att.astype(F32), axis=1, keepdims=True)
    ds = (p * (dp_ref[...] - delta)).astype(BF)
    dq_ref[...] = (dq0_ref[...] + (nn(ds, k_ref[...]) * SCALE + nn(e, first)) * own32).astype(BF)
    dk_ref[...] = (dk0_ref[...] + tn(ds, q_own) * SCALE + nn(dkv, first) * own32).astype(BF)
    dv_ref[...] = (dv0_ref[...] + tn(p.astype(BF), ga_own) + nn(dkv, second) * own32).astype(BF)


def call(kernel, inputs, outs, scratch=(), scalars=False, near=(), keep=(), limit=LIMIT, **more):
    vmem = pl.BlockSpec(memory_space=pltpu.VMEM)
    put = pltpu.with_memory_space_constraint
    placed = [put(x, pltpu.VMEM if n in near else pltpu.HBM) for n, x in enumerate(inputs)]
    specs = [vmem] * len(inputs)
    if scalars:
        placed[0], specs[0] = inputs[0], pl.BlockSpec(memory_space=pltpu.SMEM)
    settings = dict(in_specs=specs, out_specs=[vmem] * len(outs))
    settings.update(more)
    return pl.pallas_call(
        kernel,
        out_shape=[(pltpu.VMEM if n in keep else pltpu.HBM)(s, t) for n, (s, t) in enumerate(outs)],
        scratch_shapes=[pltpu.VMEM(s, t) for s, t in scratch],
        compiler_params=pltpu.CompilerParams(vmem_limit_bytes=limit * 1024 * 1024),
        **settings,
    )(*placed)


def on_device(query_rows, key_rows, value_rows, grad_out, out_weight, tile_counts):
    q, k, v, g = query_rows[0], key_rows[0], value_rows[0], grad_out[0]
    place = lax.axis_index("seq")
    other_core = [(0, 1), (1, 0), (2, 3), (3, 2)]
    flat, tall = (ROWS, WIDTH), (WIDTH, ROWS)

    send, count = call(
        pack_kernel, (tile_counts, q, k, v, g), [((PEERS, SEND_ROWS, LANES), BF), ((8, LANES), jnp.int32)],
        [((PEERS * 16 + 64, LANES), F32), ((PEERS * 24 + 96, LANES), F32)], keep=(0, 1), scalars=True,
    )
    x = lax.all_to_all(send, "seq", 0, 0)

    part = (PEERS, PART_ROWS, LANES)
    at0, lse0, keep, swap = call(
        forward_kernel, (count, q, k, v, g), [(tall, BF), ((2 * HEADS, ROWS), F32), (part, BF), (part, BF)],
        [(tall, BF), (tall, BF), ((6, WIDTH + 16, LANES), F32), (((PEERS + 1) * PART_ROWS, LANES), F32)],
        near=(0,),
    )
    got = lax.ppermute(swap, "slide", other_core)
    (joined,) = call(join_kernel, (keep, got), [((PEERS, BACK_ROWS, LANES), BF)], keep=(0,))

    w_head = lax.dynamic_slice_in_dim(out_weight, place // 4 * HEAD_WIDTH, HEAD_WIDTH, 0)
    held = pl.BlockSpec(memory_space=pltpu.VMEM)
    whole = lambda *shape: pl.BlockSpec(shape, lambda i: (0,) * len(shape))
    back, strided = call(
        far_kernel,
        (count, x, w_head, joined),
        [((PEERS, BACK_ROWS, LANES), BF), ((4, 12, WIDTH), F32)],
        [(((PEERS + 1) * n, LANES), F32) for n in (16, 24, 16)],
        near=(0, 1, 2, 3),
        keep=(0,),
        grid=(1,),
        in_specs=[
            whole(8, LANES),
            whole(PEERS, SEND_ROWS, LANES),
            whole(HEAD_WIDTH, WIDTH),
            pl.BlockSpec(memory_space=pl.ANY),
        ],
        out_specs=[whole(PEERS, 16, LANES), whole(4, 12, WIDTH)],
        input_output_aliases={3: 0},
    )
    y = lax.all_to_all(back, "seq", 0, 0)

    dq0, dk0, dv0, layer0, ga, s0, dp0, strided = call(
        backward_kernel, (count, q, k, v, g, out_weight, at0, lse0, strided),
        [(flat, F32)] * 4 + [(flat, BF)] + [((ROWS, ROWS), F32)] * 2 + [((4, 12, WIDTH), F32)],
        [(tall, BF)] * 3 + [(tall, F32)] * 3,
        near=(0,),
        keep=(0, 1, 2),
    )
    quarter = place % 4
    pieces = []
    for step in range(4):
        mine = lax.dynamic_index_in_dim(strided, (quarter + step) % 4, 0, keepdims=False)
        ring = [(d, d // 4 * 4 + (d + step) % 4) for d in range(PEERS)]
        pieces.append(lax.ppermute(mine, "seq", ring) if step else mine)
    (weight,) = call(
        weight_kernel, (y, *pieces), [((12, WIDTH), F32)], [((PART_ROWS + 8, LANES), F32)], near=(0, 1, 2, 3, 4), keep=(0,)
    )
    others = [lax.ppermute(weight, "slide", [(n, n ^ bits) for n in range(4)]) for bits in (2, 3, 1)]

    outs = call(
        final_kernel,
        (count, q, k, out_weight, y, s0, dp0, ga, layer0, dq0, dk0, dv0),
        [(flat, BF)] * 4,
        [((PEERS * 16 + 64, LANES), F32)],
        near=(0, 4, 9, 10, 11),
        grid=(1,),
        in_specs=[held] * 4 + [whole(PEERS, 16, LANES)] + [held] * 7,
    )
    return tuple(o[None] for o in outs) + (weight + others[0] + others[1] + others[2],)


def solution(mesh):
    rows = P("slide", "seq", None)
    return jax.shard_map(
        on_device,
        mesh=mesh,
        in_specs=(rows, rows, rows, rows, P(), P("slide")),
        out_specs=(rows, rows, rows, rows, P("seq", None)),
        check_vma=False,
    )
```
